32 devices in a mesh: dp: 8 (over z, y), vocab: 4 (over x, core).
Axes of the slice: x: 2, y: 2, z: 4, core: 2. Of those that a mesh axis runs over, the one named last changes fastest.
Arguments:
- hidden: bfloat16 [6144, 2048], P('dp', 'vocab')
- gain: bfloat16 [2048], replicated, may hold values from 0.5 to 1.5
- head: bfloat16 [2048, 32000], P('dp', 'vocab')
- target_ids: int32 [6144], P('dp'), may hold values from 0 to 31999
- seq_lens: int32 [16], replicated, may hold values from 64 to 704, as said below
- seq_owner: int32 [16], replicated, may hold values from 0 to 7, as said below
Outputs:
- logprob: float32 [6144], P('dp')
- entropy: float32 [6144], P('dp')
The draws below stay inside these ranges and needn't reach their ends.
Inputs may be any that keep to these rules, and one draw needn't show every extreme that they name: `seq_lens`: the lengths of the sequences owned by one dp index sum to at most 768; in every draw the sequences of some dp index sum to exactly 768. `seq_owner`: every dp index owns exactly 2 sequences.
All inputs are finite; a program needn't handle non-finite values.
Results may differ from the reference program's by a relative error of at most 0.0075.
Values may be sent and summed in bfloat16 or wider, within the bound.
No kernel may reach another device: no remote copies, remote signals or barrier semaphores. Data moves between devices by JAX's collectives and lax.ppermute only.
A program may use at most 128 MiB of HBM per device.

```python
import math
import jax
import jax.numpy as jnp
import numpy as np
from jax import lax

D = 2048
V = 32000
CAP = 768
SEQ_DEV = 2
SEQS = 16
TOKENS = 6144
N_DP = 8


def shared_direction(key):
    return jax.random.truncated_normal(jax.random.fold_in(key, 9), -4.0, 4.0, (D,), jnp.float32) / math.sqrt(D)


def head_spread():
    spread = 3.0
    return spread


def head_values(key):
    spread = head_spread()
    noise = jax.random.truncated_normal(jax.random.fold_in(key, 3), -5.0, 5.0, (D, V), jnp.float32)
    amplitude = 300.0 / math.sqrt(D)
    return noise * (spread / math.sqrt(D)) + amplitude * shared_direction(key)[:, None]


def draw_head(key, part):
    return head_values(key).astype(jnp.bfloat16)


def draw_hidden(key, part):
    spread = head_spread()
    base = jax.random.truncated_normal(jax.random.fold_in(key, 5), -4.0, 4.0, (TOKENS, D), jnp.float32)
    row_scale = jnp.exp(jax.random.uniform(jax.random.fold_in(key, 6), (TOKENS, 1), jnp.float32) * math.log(10.0))
    col_scale = jnp.exp(jax.random.uniform(jax.random.fold_in(key, 7), (1, D), jnp.float32) * math.log(10.0))
    values = base * row_scale * col_scale
    weights = head_values(key)
    direction = shared_direction(key)
    row_index = jnp.arange(TOKENS, dtype=jnp.int32)
    first = row_index * 7919 % V
    second = (first + V // 2 + 1) % V
    paired = jnp.take(weights, first, axis=1).T + 0.98 * jnp.take(weights, second, axis=1).T
    strength = jnp.where(row_index % 3 == 0, 0.0, jnp.where(row_index % 3 == 1, 0.3, 0.6))
    lift = spread * (1.0 + 0.5 * (row_index // 61 % 3).astype(jnp.float32))
    aligned = (paired + strength[:, None] * base * (spread / math.sqrt(D)) + lift[:, None] * direction[None, :]) * row_scale
    chosen = row_index % 61 == 0
    values = jnp.where(chosen[:, None], aligned, values)
    return values.astype(jnp.bfloat16)


def sequence_plan(key):
    base = jax.random.fold_in(key, 17)
    order = jax.random.permutation(jax.random.fold_in(base, 1), SEQS).astype(jnp.int32)
    shorts = jax.random.randint(jax.random.fold_in(base, 2), (SEQS,), CAP // 6, CAP // 3 + 1, dtype=jnp.int32)
    devices = SEQS // SEQ_DEV
    flags = jax.random.randint(jax.random.fold_in(base, 3), (devices,), 0, 8, dtype=jnp.int32) == 0
    forced = jax.random.randint(jax.random.fold_in(base, 4), (), 0, devices, dtype=jnp.int32)
    device_index = jnp.arange(devices, dtype=jnp.int32)
    first = jnp.where(device_index == forced, CAP // 12, shorts[0::2])
    second = jnp.where(flags, CAP - first, shorts[1::2])
    second = jnp.where(device_index == forced, CAP - CAP // 12, second)
    by_slot = jnp.stack([first, second], axis=1).reshape(SEQS)
    lengths = by_slot[order]
    owners = order // SEQ_DEV
    return (lengths.astype(jnp.int32), owners.astype(jnp.int32))


def draw_seq_lens(key, part):
    return sequence_plan(key)[0]


def draw_seq_owner(key, part):
    return sequence_plan(key)[1]


def with_ends(drawn, own_key, least, largest):
    index_at = [jax.random.randint(jax.random.fold_in(own_key, axis), (), 0, length) for axis, length in enumerate(drawn.shape)]
    main_axis = drawn.shape.index(max(drawn.shape))
    neighbour = index_at[:main_axis] + [(index_at[main_axis] + 1) % drawn.shape[main_axis]] + index_at[main_axis + 1:]
    return drawn.at[tuple(index_at)].set(least).at[tuple(neighbour)].set(largest)


def cumulative_ranks(amount, slope):
    weights = [(1 << 20) // math.isqrt(rank ** slope) + 1 for rank in range(1, amount + 1)]
    width = 1 + sum(weights) // (1 << 30)
    return np.cumsum(np.array([max(1, weight // width) for weight in weights]))


def ranked_ids(own_key, extent, count, lean):
    table = cumulative_ranks(count, lean)
    ticket = jax.random.randint(jax.random.fold_in(own_key, 1), extent, 0, int(table[count - 1]))
    standing = jnp.searchsorted(jnp.asarray(table, jnp.int32), ticket, side="right")
    return jax.random.permutation(jax.random.fold_in(own_key, 2), count)[standing].astype(jnp.int32)


def setup_inputs(seed: int = 0) -> dict:
    key_of = jax.random.split(jax.random.key(seed), 7)
    hidden = draw_hidden(jax.random.fold_in(key_of[6], 71), 0)
    gain = jnp.clip(1.0 + 0.1 * jax.random.normal(key_of[1], (D,), jnp.float32), 0.5, 1.5).astype(jnp.bfloat16)
    head = draw_head(jax.random.fold_in(key_of[6], 71), 0)
    target_ids = with_ends(ranked_ids(key_of[3], (TOKENS,), V, 2), jax.random.fold_in(key_of[3], 3), 0, V - 1).astype(jnp.int32)
    seq_lens = draw_seq_lens(jax.random.fold_in(key_of[6], 71), 0)
    seq_owner = draw_seq_owner(jax.random.fold_in(key_of[6], 71), 0)
    return dict(hidden=hidden, gain=gain, head=head, target_ids=target_ids, seq_lens=seq_lens, seq_owner=seq_owner)


EPS = 1e-05

def reference(hidden, gain, head, target_ids, seq_lens, seq_owner):
    owners = jnp.arange(N_DP, dtype=jnp.int32)
    loads = lax.optimization_barrier(jnp.sum(jnp.where(seq_owner[:, None] == owners[None, :], seq_lens[:, None], 0), axis=0)).astype(jnp.int32)
    slot_index = jnp.arange(TOKENS, dtype=jnp.int32)
    live = slot_index % CAP < loads[(slot_index // CAP).astype(jnp.int32)]
    wide = hidden.astype(jnp.float32)
    normed = (wide * lax.rsqrt(lax.optimization_barrier(jnp.mean(wide * wide, axis=1, keepdims=True)) + EPS) * gain.astype(jnp.float32)).astype(jnp.bfloat16)
    weight_full = head.astype(jnp.float32)
    block_rows = min(128, CAP)

    def scored(block_norm, block_ids):
        logits = jnp.dot(block_norm.astype(jnp.float32), weight_full, precision=lax.Precision.HIGHEST)
        top = lax.optimization_barrier(jnp.max(logits, axis=1))
        expo = jnp.exp(logits - top[:, None])
        total = lax.optimization_barrier(jnp.sum(expo, axis=1))
        weighted = lax.optimization_barrier(jnp.sum(expo * logits, axis=1))
        lse = top + jnp.log(total)
        picked = jnp.take_along_axis(logits, block_ids[:, None], axis=1)[:, 0]
        return (picked - lse, lse - weighted / total)

    def skipped(block_norm, block_ids):
        zeros = jnp.zeros((block_rows,), jnp.float32)
        return (zeros, zeros)

    def per_block(item):
        block_norm, block_ids, block_live = item
        return lax.cond(jnp.any(block_live), scored, skipped, block_norm, block_ids)
    blocks = TOKENS // block_rows
    log_part, ent_part = lax.map(per_block, (normed.reshape(blocks, block_rows, D), target_ids.reshape(blocks, block_rows), live.reshape(blocks, block_rows)))
    logprob = jnp.where(live, log_part.reshape(TOKENS), 0.0)
    entropy = jnp.where(live, ent_part.reshape(TOKENS), 0.0)
    return (logprob, entropy)
```

```python
import functools

import jax
import jax.numpy as jnp
from jax import lax
from jax.experimental import pallas as pl
from jax.experimental.pallas import tpu as pltpu
from jax.sharding import PartitionSpec as P

EPS = 1e-05
LOW = -3.0e38
LANES = 128
TILE = 16
PIECES = (8, 7, 6, 4)
ROWS = 256
TOKEN_BYTES = 17 * 2**20


def assemble_kernel(count, place, gain_ref, *refs):
    target = refs[-1]
    sources = [(ref, index) for ref in refs[:count] for index in range(ref.shape[1])]
    features = refs[0].shape[3]
    for start in range(0, target.shape[3], LANES):
        lanes = slice(start, start + LANES)
        square = sum(
            jnp.sum(jnp.square(ref[0, at, lanes].astype(jnp.float32)), axis=1, keepdims=True) for ref, at in sources
        )
        scale = lax.rsqrt(square / (features * len(sources)) + EPS)
        for number, (ref, at) in enumerate(sources):
            first = pl.multiple_of((place[0] ^ place[1 + number]) * features, features)
            value = ref[0, at, lanes].astype(jnp.float32) * scale * gain_ref[:, pl.ds(first, features)]
            target[0, 0, pl.ds(first, features), lanes] = value.T.astype(target.dtype)


def assemble(part, offsets, gain, sources, rows, at, groups, splits, whole):
    count, _, _, features = sources[0].shape
    wide = features * len(offsets)
    place = jnp.stack([part] + [jnp.int32(offset) for offset in offsets]).astype(jnp.int32)
    before = [] if whole is None else [whole]
    return pl.pallas_call(
        functools.partial(assemble_kernel, len(sources)),
        grid_spec=pltpu.PrefetchScalarGridSpec(
            num_scalar_prefetch=1,
            grid=(count, splits),
            in_specs=[pl.BlockSpec((1, wide), lambda i, j, s: (0, 0))]
            + [pl.BlockSpec((1, y.shape[1], rows, features), lambda i, j, s: (i, 0, j, 0)) for y in sources]
            + [pl.BlockSpec(memory_space=pl.ANY)] * len(before),
            out_specs=pl.BlockSpec((1, 1, wide, rows), lambda i, j, s: (at + i, j, 0, 0)),
        ),
        out_shape=jax.ShapeDtypeStruct((groups, splits, wide, rows), sources[0].dtype),
        input_output_aliases={2 + len(sources): 0} if before else {},
        compiler_params=pltpu.CompilerParams(vmem_limit_bytes=24 * 2**20),
        cost_estimate=pl.CostEstimate(
            flops=6 * count * splits * rows * wide,
            bytes_accessed=4 * count * splits * rows * wide,
            transcendentals=count * splits * rows,
        ),
    )(place, gain, *sources, *before)


def stats_kernel(masked, scalars, *refs):
    x_ref, ids_ref = refs[:2]
    head_refs, (out_ref, head, logits, sems) = refs[2:-4], refs[-4:]
    step = pl.program_id(0)
    live = scalars[0]
    rows = x_ref.shape[3]
    count, width, depth = head_refs[0].shape

    @pl.when(step == 0)
    def _():
        copies = []
        for away, source in enumerate(head_refs):
            for index in range(count):
                start = pl.multiple_of((index * len(head_refs) + (scalars[2] ^ away)) * depth, depth)
                copies.append(
                    pltpu.make_async_copy(source.at[index], head.at[:, pl.ds(start, depth)], sems.at[len(copies)])
                )
        for copy in copies:
            copy.start()
        for copy in copies:
            copy.wait()

    def multiply():
        logits[lax.rem(step, 2)] = lax.dot_general(
            head[...], x_ref[0, 0], (((1,), (0,)), ((), ())), preferred_element_type=jnp.float32
        )

    def reduce():
        slot = lax.rem(step + 1, 2)
        column = lax.broadcasted_iota(jnp.int32, (width, LANES), 0)
        for start in range(0, rows, LANES):
            lanes = slice(start, start + LANES)
            block = logits[slot, :, lanes]
            if masked:
                block = jnp.where(column < scalars[1], block, LOW)
            top = jnp.max(block, axis=0, keepdims=True)
            shifted = jnp.maximum(block - top, -1.0e4)
            expo = jnp.exp(shifted)
            out_ref[0, 0:1, lanes] = top
            out_ref[0, 1:2, lanes] = jnp.sum(expo, axis=0, keepdims=True)
            out_ref[0, 2:3, lanes] = jnp.sum(expo * shifted, axis=0, keepdims=True)
            out_ref[0, 3:4, lanes] = jnp.sum(
                jnp.where(column == ids_ref[0, :, lanes], block, 0.0), axis=0, keepdims=True
            )

    @pl.when(step == 0)
    def _():
        multiply()

    @pl.when((step > 0) & (step < live))
    def _():
        multiply()
        reduce()

    @pl.when(step == live)
    def _():
        reduce()


def stats(alive, real, low, x, ids, heads, masked):
    groups, per, wide, rows = x.shape
    blocks = groups * per
    count, width, depth = heads[0].shape
    order = jnp.argsort(jnp.logical_not(alive))
    number = jnp.sum(alive.astype(jnp.int32))
    scalars = jnp.concatenate([jnp.stack([number, real, low]), order]).astype(jnp.int32)

    def here(i, s):
        return s[3 + jnp.minimum(i, s[0] - 1)]

    def before(i, s):
        return s[3 + jnp.minimum(jnp.maximum(i - 1, 0), s[0] - 1)]

    return pl.pallas_call(
        functools.partial(stats_kernel, masked),
        grid_spec=pltpu.PrefetchScalarGridSpec(
            num_scalar_prefetch=1,
            grid=(blocks + 1,),
            in_specs=[
                pl.BlockSpec((1, 1, wide, rows), lambda i, s: (here(i, s) // per, here(i, s) % per, 0, 0)),
                pl.BlockSpec((1, 1, rows), lambda i, s: (before(i, s), 0, 0)),
            ]
            + [pl.BlockSpec(memory_space=pl.ANY)] * len(heads),
            out_specs=pl.BlockSpec((1, 4, rows), lambda i, s: (before(i, s), 0, 0)),
            scratch_shapes=[
                pltpu.VMEM((width, wide), jnp.bfloat16),
                pltpu.VMEM((2, width, rows), jnp.float32),
                pltpu.SemaphoreType.DMA((count * len(heads),)),
            ],
        ),
        out_shape=jax.ShapeDtypeStruct((blocks, 4, rows), jnp.float32),
        compiler_params=pltpu.CompilerParams(vmem_limit_bytes=32 * 2**20),
        cost_estimate=pl.CostEstimate(
            flops=2 * blocks * rows * wide * width,
            bytes_accessed=x.size * 2 + wide * width * 2,
            transcendentals=blocks * rows * width,
        ),
    )(scalars, x, ids, *heads)


def merge(members):
    top, total, weighted, picked = (jnp.stack([m[..., i, :] for m in members]) for i in range(4))
    best = jnp.max(top, axis=0)
    shift = jnp.maximum(top - best[None], -1.0e4)
    factor = jnp.exp(shift)
    return jnp.stack(
        [
            best,
            jnp.sum(total * factor, axis=0),
            jnp.sum(factor * (weighted + total * shift), axis=0),
            jnp.sum(picked, axis=0),
        ],
        axis=-2,
    )


def by_collectives(hidden, gain, head, target_ids, loads):
    groups = lax.axis_size("dp")
    parts = lax.axis_size("vocab")
    slots, features = hidden.shape
    depth, breadth = head.shape
    width = -(-breadth // (groups * TILE)) * TILE
    base = lax.axis_index("dp") * width
    real = jnp.clip(breadth - base, 0, width)
    places = lax.all_gather(target_ids, "dp", axis=0) - (lax.axis_index("vocab") * breadth + base)
    places = jnp.where(places < real, places, -1)

    spread = jnp.pad(head.T, ((0, groups * width - breadth), (0, 0))).reshape(groups, width, depth)
    columns = lax.all_to_all(spread, "dp", split_axis=0, concat_axis=0, tiled=True)
    columns = columns.transpose(1, 0, 2).reshape(1, width, groups * depth)

    splits = -(-groups * slots * features * parts * 2 // TOKEN_BYTES)
    while slots % splits or (slots // splits) % LANES:
        splits += 1
    rows = slots // splits
    zero = jnp.int32(0)
    results = []
    for start in range(0, slots, rows):
        piece = hidden[start : start + rows]
        if results:
            piece, _ = lax.optimization_barrier((piece, results[-1]))
        x = lax.all_gather(piece, ("dp", "vocab"), axis=0).reshape(groups, parts, rows, features)
        x = assemble(zero, tuple(range(parts)), gain, [x], rows, 0, groups, 1, None)
        ids = places[:, None, start : start + rows]
        results.append(stats(start < loads, real, zero, x, ids, [columns], True))
    found = lax.all_to_all(jnp.concatenate(results, axis=2), "dp", split_axis=0, concat_axis=0, tiled=True)
    mine = lax.all_gather(merge(list(found)), "vocab", axis=0)
    return merge(list(mine))


def by_axes(hidden, gain, head, target_ids, loads):
    groups = lax.axis_size("dp")
    parts = lax.axis_size("vocab")
    position = lax.axis_index("dp")
    part = lax.axis_index("vocab")
    tall = groups // 2
    hi = position // 2
    low = position % 2
    slots, features = hidden.shape
    depth, breadth = head.shape
    chunk = breadth // tall
    ends = [chunk * sum(PIECES[:n]) // sum(PIECES) // TILE * TILE for n in range(len(PIECES))] + [chunk]
    cuts = [(start, end - start) for start, end in zip(ends, ends[1:])]
    lines = [[2 * index + side for index in range(tall)] for side in range(2)]

    def swap_hi(x, step):
        return lax.ppermute(x, "dp", [(g, g ^ (2 * step)) for g in range(groups)])

    def swap_lo(x):
        return lax.ppermute(x, "dp", [(g, g ^ 1) for g in range(groups)])

    def swap_part(x, step):
        return lax.ppermute(x, "vocab", [(v, v ^ step) for v in range(parts)])

    def along(x, moves):
        return lax.ppermute(x, "dp", [(2 * a + side, 2 * b + side) for a, b in moves for side in range(2)])

    turned = head.T.reshape(tall, chunk, depth)
    heads = []
    for start, width in cuts:
        mine = lax.all_to_all(
            turned[:, start : start + width], "dp", split_axis=0, concat_axis=0, axis_index_groups=lines, tiled=True
        )
        heads.append([mine, swap_lo(mine)])

    code = jnp.concatenate([target_ids >> 8, target_ids & 255]).astype(hidden.dtype)
    code = jnp.pad(code, (0, TILE * features - 2 * slots)).reshape(TILE, features)
    own = jnp.concatenate([hidden, code])
    middle = (hi == 1) | (hi == 2)
    near = swap_hi(own, 1)
    cross = along(own, [(1, 2), (2, 1)])
    cross_near = along(near, [(1, 2), (2, 1)])
    out = along(cross, [(1, 0), (2, 3)])
    out_near = along(cross_near, [(1, 0), (2, 3)])
    order = [0, 1, jnp.where(middle, 3, 2), jnp.where(middle, 2, 3)]
    splits = slots // ROWS
    x = None
    codes = []
    for index, y in enumerate([own, near, jnp.where(middle, cross, out), jnp.where(middle, cross_near, out_near)]):
        held = [y]
        offsets = [0]
        for step in (2, 1):
            held = held + [swap_part(z, step) for z in held]
            offsets = offsets + [offset ^ step for offset in offsets]
        x = assemble(part, offsets, gain, [z[None, None] for z in held], ROWS, index, tall, splits, x)
        codes.append(y[slots:].reshape(TILE * features)[: 2 * slots].astype(jnp.int32))
    code = jnp.stack(codes)
    ids = (code[:, :slots] * 256 + code[:, slots:]).reshape(tall * splits, 1, ROWS)

    first = jnp.arange(splits, dtype=jnp.int32) * ROWS
    own_loads = loads[2 * (hi ^ jnp.stack([jnp.int32(away) for away in order])) + low]
    alive = (first[None, :] < own_loads[:, None]).reshape(-1)
    found = []
    for (start, width), members in zip(cuts, heads):
        places = ids - (part * breadth + hi * chunk + start)
        places = jnp.where(places < width, places, -1)
        found.append(stats(alive, jnp.int32(width), low, x, places, members, False))
    found = merge(found).reshape(tall, splits, 4, ROWS).transpose(0, 2, 1, 3).reshape(tall, 4, slots)

    def of(step):
        return lax.dynamic_index_in_dim(found, order[step], keepdims=False)

    mine = merge([of(0)] + [swap_hi(of(step), step) for step in range(1, tall)])
    return merge([mine] + [swap_part(mine, step) for step in range(1, parts)])


def local(hidden, gain, head, target_ids, seq_lens, seq_owner):
    groups = lax.axis_size("dp")
    slots, features = hidden.shape
    owners = jnp.arange(groups, dtype=jnp.int32)
    loads = jnp.sum(jnp.where(seq_owner[:, None] == owners[None, :], seq_lens[:, None], 0), axis=0).astype(jnp.int32)
    fits = (
        (groups, lax.axis_size("vocab")) == (8, 4)
        and slots % ROWS == 0
        and 2 * slots <= TILE * features
        and head.shape[1] % (groups // 2 * TILE) == 0
    )
    transport = by_axes if fits else by_collectives
    scores = transport(hidden, gain.astype(jnp.float32)[None], head, target_ids, loads)
    top, total, weighted, picked = (scores[index] for index in range(4))
    spread = jnp.log(total)
    logprob = picked - (top + spread)
    entropy = spread - weighted / total
    live = jnp.arange(slots, dtype=jnp.int32) < loads[lax.axis_index("dp")]
    return (jnp.where(live, logprob, 0.0), jnp.where(live, entropy, 0.0))


def solution(mesh):
    return jax.shard_map(
        local,
        mesh=mesh,
        in_specs=(P("dp", "vocab"), P(), P("dp", "vocab"), P("dp"), P(), P()),
        out_specs=(P("dp"), P("dp")),
        check_vma=False,
    )
```

```python
import functools

import jax
import jax.numpy as jnp
from jax import lax
from jax.experimental import pallas as pl
from jax.experimental.pallas import tpu as pltpu
from jax.sharding import PartitionSpec as P

EPS = 1e-05
LOW = -3.0e38
LANES = 128
TILE = 16
PIECES = (8, 7, 5)
ROWS = 256
TOKEN_BYTES = 17 * 2**20


def assemble_kernel(near_first, gain_ref, *refs):
    target = refs[-1]
    sources = []
    for away, ref in enumerate(refs[:-1]):
        for index in range(ref.shape[0]):
            part = lax.axis_index("vocab") ^ (2 * index + away) if near_first else index
            sources.append((ref, index, part))
    features = refs[0].shape[3]
    for start in range(0, target.shape[3], LANES):
        lanes = slice(start, start + LANES)
        square = sum(
            jnp.sum(jnp.square(ref[at, 0, lanes].astype(jnp.float32)), axis=1, keepdims=True) for ref, at, _ in sources
        )
        scale = lax.rsqrt(square / (features * len(sources)) + EPS)
        for ref, at, part in sources:
            first = pl.multiple_of(part * features, features)
            value = ref[at, 0, lanes].astype(jnp.float32) * scale * gain_ref[:, pl.ds(first, features)]
            target[0, 0, pl.ds(first, features), lanes] = value.T.astype(target.dtype)


def assemble(gain, sources, rows):
    _, count, slots, features = sources[0].shape
    splits = slots // rows
    wide = features * sum(y.shape[0] for y in sources)
    return pl.pallas_call(
        functools.partial(assemble_kernel, len(sources) > 1),
        grid=(count, splits),
        in_specs=[pl.BlockSpec((1, wide), lambda i, j: (0, 0))]
        + [pl.BlockSpec((y.shape[0], 1, rows, features), lambda i, j: (0, i, j, 0)) for y in sources],
        out_specs=pl.BlockSpec((1, 1, wide, rows), lambda i, j: (i, j, 0, 0)),
        out_shape=jax.ShapeDtypeStruct((count, splits, wide, rows), sources[0].dtype),
        compiler_params=pltpu.CompilerParams(vmem_limit_bytes=24 * 2**20),
        cost_estimate=pl.CostEstimate(
            flops=6 * count * splits * rows * wide,
            bytes_accessed=4 * count * splits * rows * wide,
            transcendentals=count * splits * rows,
        ),
    )(gain, *sources)


def stats_kernel(plan, counts, start_ref, lens_ref, owner_ref, *refs):
    out_ref, head, held, logits, ids, order, sems, token_sems = refs[-8:]
    members = []
    for count in counts:
        members.append(refs[:count])
        refs = refs[count:]
    token_refs, id_refs, head_refs, before = members
    splits, _, rows = token_refs[0].shape[1:]
    groups = len(token_refs) * token_refs[0].shape[0]
    width, depth = head.shape[0], head_refs[0].shape[-1]
    real, base = plan.columns()

    copies = []
    for source, group in plan.head_parts(head_refs):
        lane = pl.multiple_of(group * depth, LANES)
        copies.append(pltpu.make_async_copy(source, head.at[:, pl.ds(lane, depth)], sems.at[len(copies)]))
    for copy in copies:
        copy.start()

    def one_group(group, live):
        def one_sequence(index, load):
            return load + jnp.where(owner_ref[index] == plan.group(group), lens_ref[index], 0)

        load = lax.fori_loop(0, lens_ref.shape[0], one_sequence, jnp.int32(0))
        for split in range(splits):
            order[live] = group * splits + split
            live = live + jnp.where(start_ref[0] + split * rows < load, 1, 0)
        return live

    live = lax.fori_loop(0, groups, one_group, jnp.int32(0))

    def fetch(step, slot):
        group, split = order[step] // splits, order[step] % splits
        each = token_refs[0].shape[0]
        for index, source in enumerate(token_refs):

            @pl.when(group // each == index)
            def _():
                pltpu.make_async_copy(source.at[group % each, split], held.at[slot], token_sems.at[slot]).start()

    @pl.when(live > 0)
    def _():
        fetch(0, 0)

    out_ref[...] = jnp.zeros_like(out_ref)
    for index, source in enumerate(id_refs):
        places = source[...] - base
        ids[pl.ds(index * source.shape[0], source.shape[0])] = jnp.where(places < real, places, -1)
    for copy in copies:
        copy.wait()

    def body(step, carry):
        slot = lax.rem(step, 2)
        pltpu.make_async_copy(token_refs[0].at[0, 0], held.at[slot], token_sems.at[slot]).wait()

        @pl.when(step + 1 < live)
        def _():
            fetch(step + 1, 1 - slot)

        logits[...] = jnp.dot(head[...], held[slot], preferred_element_type=jnp.float32)

        @pl.when(real < width)
        def _():
            column = lax.broadcasted_iota(jnp.int32, (width - plan.least, rows), 0) + plan.least
            logits[plan.least :] = jnp.where(column < real, logits[plan.least :], LOW)

        block = order[step]
        target = plan.slot(block // splits)
        split = block % splits
        column = lax.broadcasted_iota(jnp.int32, (width, LANES), 0)
        for start in range(0, rows, LANES):
            lanes = slice(start, start + LANES)
            values = logits[:, lanes]
            top = jnp.max(values, axis=0, keepdims=True)
            shifted = jnp.maximum(values - top, -1.0e4)
            expo = jnp.exp(shifted)
            total = jnp.sum(expo, axis=0, keepdims=True)
            weighted = jnp.sum(expo * shifted, axis=0, keepdims=True)
            picked = jnp.sum(jnp.where(column == ids[block, :, lanes], values, 0.0), axis=0, keepdims=True)
            place = pl.ds(pl.multiple_of(split * rows + start, LANES), LANES)
            if before:
                top, total, weighted, picked = joined(
                    [(top, total, weighted, picked), [before[0][target, index : index + 1, place] for index in range(4)]]
                )
            for index, member in enumerate((top, total, weighted, picked)):
                out_ref[target, index : index + 1, place] = member
        return carry

    lax.fori_loop(0, live, body, 0)


def stats(plan, start, seq_lens, seq_owner, tokens, ids, heads, before):
    groups, splits, wide, rows = tokens[0].shape
    groups *= len(tokens)
    width = plan.width
    smem = pl.BlockSpec(memory_space=pltpu.SMEM)
    vmem = pl.BlockSpec(memory_space=pltpu.VMEM)
    anywhere = pl.BlockSpec(memory_space=pl.ANY)
    return pl.pallas_call(
        functools.partial(stats_kernel, plan, (len(tokens), len(ids), len(heads), len(before))),
        in_specs=[smem] * 3
        + [anywhere] * len(tokens)
        + [vmem] * len(ids)
        + [anywhere] * len(heads)
        + [vmem] * len(before),
        out_specs=vmem,
        scratch_shapes=[
            pltpu.VMEM((width, wide), jnp.bfloat16),
            pltpu.VMEM((2, wide, rows), jnp.bfloat16),
            pltpu.VMEM((width, rows), jnp.float32),
            pltpu.VMEM((groups * splits, 1, rows), jnp.int32),
            pltpu.SMEM((groups * splits + 1,), jnp.int32),
            pltpu.SemaphoreType.DMA((wide // heads[0].shape[-1],)),
            pltpu.SemaphoreType.DMA((2,)),
        ],
        out_shape=jax.ShapeDtypeStruct((groups, 4, splits * rows), jnp.float32),
        compiler_params=pltpu.CompilerParams(vmem_limit_bytes=24 * 2**20),
        cost_estimate=pl.CostEstimate(
            flops=2 * groups * splits * rows * wide * width,
            bytes_accessed=groups * splits * rows * wide * 2 + wide * width * 2,
            transcendentals=groups * splits * rows * width,
        ),
    )(start, seq_lens, seq_owner, *tokens, *ids, *heads, *before)


class Spread:
    def __init__(self, breadth, groups):
        self.breadth = breadth
        self.cuts = [breadth * index // groups // TILE * TILE for index in range(groups)] + [breadth]
        sizes = [end - start for start, end in zip(self.cuts, self.cuts[1:])]
        self.width, self.least = max(sizes), min(sizes)

    def spread(self, turned):
        turned = jnp.pad(turned, ((0, self.cuts[-2] + self.width - self.breadth), (0, 0)))
        return jnp.stack([turned[start : start + self.width] for start in self.cuts[:-1]])

    def columns(self):
        position = lax.axis_index("dp")
        start, end = 0, self.breadth
        for index, (first, last) in enumerate(zip(self.cuts, self.cuts[1:])):
            start = jnp.where(position == index, first, start)
            end = jnp.where(position == index, last, end)
        return end - start, lax.axis_index("vocab") * self.breadth + start

    def head_parts(self, refs):
        return [(refs[0], 0)]

    def group(self, group):
        return group

    def slot(self, group):
        return group


class Line:
    def __init__(self, breadth, chunk, start, width):
        self.breadth, self.chunk, self.start = breadth, chunk, start
        self.width = self.least = width

    def columns(self):
        hi = lax.axis_index("dp") // 2
        return self.width, lax.axis_index("vocab") * self.breadth + hi * self.chunk + self.start

    def head_parts(self, refs):
        position = lax.axis_index("dp")
        hi, low = position // 2, position % 2
        here = pl.ds(self.start, self.width)
        mine = [refs[0].at[hi, here], *refs[2:5]]
        other = [refs[1].at[here], *(refs[5].at[index] for index in range(3))]
        found = [(source, 2 * (hi ^ step) + low) for step, source in enumerate(mine)]
        return found + [(source, 2 * (hi ^ step) + (low ^ 1)) for step, source in enumerate(other)]

    def slot(self, group):
        hi = lax.axis_index("dp") // 2
        middle = (hi == 1) | (hi == 2)
        return jnp.where(middle & (group >= 2), 5 - group, group)

    def group(self, group):
        position = lax.axis_index("dp")
        return 2 * (position // 2 ^ self.slot(group)) + position % 2


def after(x, *others):
    return lax.optimization_barrier((x, *others))[0]


def joined(members):
    best = functools.reduce(jnp.maximum, [top for top, _, _, _ in members])
    total = weighted = picked = 0.0
    for top, other_total, other_weighted, other_picked in members:
        shift = jnp.maximum(top - best, -1.0e4)
        factor = jnp.exp(shift)
        total += other_total * factor
        weighted += factor * (other_weighted + other_total * shift)
        picked += other_picked
    return best, total, weighted, picked


def merge(members):
    return jnp.stack(joined([[member[..., index, :] for index in range(4)] for member in members]), axis=-2)


def by_collectives(hidden, gain, head, target_ids, seq_lens, seq_owner):
    groups = lax.axis_size("dp")
    parts = lax.axis_size("vocab")
    slots, features = hidden.shape
    depth, breadth = head.shape
    plan = Spread(breadth, groups)
    ids = lax.all_gather(target_ids, "dp", axis=0)

    columns = lax.all_to_all(plan.spread(head.T), "dp", split_axis=0, concat_axis=0, tiled=True)
    columns = columns.transpose(1, 0, 2).reshape(plan.width, groups * depth)

    splits = -(-groups * slots * features * parts * 2 // TOKEN_BYTES)
    while slots % splits or (slots // splits) % LANES:
        splits += 1
    rows = slots // splits

    def score(start):
        piece = lax.dynamic_slice_in_dim(hidden, start, rows)
        x = lax.all_gather(piece, ("vocab", "dp"), axis=0).reshape(parts, groups, rows, features)
        x = assemble(gain, [x], rows)
        wanted = lax.dynamic_slice_in_dim(ids, start, rows, axis=1)[:, None]
        return stats(plan, start[None], seq_lens, seq_owner, [x], [wanted], [columns], [])

    found = lax.map(score, jnp.arange(splits, dtype=jnp.int32) * rows)
    found = found.transpose(1, 2, 0, 3).reshape(groups, 4, slots)
    found = lax.all_to_all(found, "dp", split_axis=0, concat_axis=0, tiled=True)
    mine = lax.all_gather(merge(list(found)), "vocab", axis=0)
    return merge(list(mine))


def by_axes(hidden, gain, head, target_ids, seq_lens, seq_owner):
    groups = lax.axis_size("dp")
    parts = lax.axis_size("vocab")
    tall = groups // 2
    hi = lax.axis_index("dp") // 2
    slots, features = hidden.shape
    depth, breadth = head.shape
    splits = slots // ROWS
    middle = (hi == 1) | (hi == 2)
    chunk = breadth // tall
    ends = [chunk * sum(PIECES[:n]) // sum(PIECES) // TILE * TILE for n in range(len(PIECES))] + [chunk]
    cuts = [(start, end - start) for start, end in zip(ends, ends[1:])]

    def swap_hi(x, step):
        return lax.ppermute(x, "dp", [(g, g ^ (2 * step)) for g in range(groups)])

    def swap_lo(x):
        return lax.ppermute(x, "dp", [(g, g ^ 1) for g in range(groups)])

    def swap_part(x, step):
        return lax.ppermute(x, "vocab", [(v, v ^ step) for v in range(parts)])

    def along(x, moves):
        return lax.ppermute(x, "dp", [(2 * a + side, 2 * b + side) for a, b in moves for side in range(2)])

    code = jnp.stack([target_ids >> 8, target_ids & 255]).astype(hidden.dtype).reshape(2, splits, ROWS)
    code = code.transpose(1, 0, 2).reshape(splits, 2 * ROWS)
    own = jnp.concatenate([hidden, jnp.pad(code, ((0, TILE - splits), (0, features - 2 * ROWS)))])
    near = swap_hi(own, 1)
    cross = along(own, [(1, 2), (2, 1)])
    cross_near = along(near, [(1, 2), (2, 1)])
    out = along(cross, [(1, 0), (2, 3)])
    out_near = along(cross_near, [(1, 0), (2, 3)])

    turned = head.T.reshape(tall, chunk, depth)

    def block(step, start, width):
        return lax.dynamic_slice(turned, (hi ^ step, start, 0), (1, width, depth))[0]

    def to_hi(cut, *others):
        return [swap_hi(after(block(step, *cut), *others), step) for step in (1, 2, 3)]

    def over_x(x):
        return swap_part(x, 2)

    def both(x, y, x_across, y_across):
        return jnp.stack([jnp.stack([x, y]), jnp.stack([x_across, y_across])])

    def ready(half, whole):
        code = half[0, :, slots : slots + splits, : 2 * ROWS].astype(jnp.int32).reshape(2 * splits, 2, ROWS)
        return assemble(gain, [half, whole], ROWS), code[:, :1] * 256 + code[:, 1:]

    def score(piece, before):
        start, width = cuts[piece]
        plan = Line(breadth, chunk, start, width)
        heads = [turned, local_block, *sent[piece], across[piece]]
        return stats(plan, jnp.zeros(1, jnp.int32), seq_lens, seq_owner, tokens, ids, heads, before)

    local_block = swap_lo(block(0, 0, chunk))
    own_across = over_x(own)
    near_across = over_x(near)
    sent = [to_hi(cuts[0], out, cross_near, local_block, own_across, near_across)]
    far = jnp.where(middle, cross, out)
    far_across = over_x(far)
    last = jnp.where(middle, cross_near, out_near)
    last_across = over_x(after(last, *sent[0]))
    front_half = both(own, near, own_across, near_across)
    front_whole = swap_part(front_half, 1)
    back_half = both(far, last, far_across, last_across)
    back_whole = swap_part(back_half, 1)
    across = [swap_lo(jnp.stack(sent[0]))]
    sent.append(to_hi(cuts[1], *sent[0], far_across))
    across.append(swap_lo(jnp.stack(sent[1])))
    tokens, ids = zip(ready(front_half, front_whole), ready(back_half, back_whole))
    sent.append(to_hi(cuts[2], *sent[1], tokens[0], last_across))
    found = score(0, [])
    across.append(swap_lo(after(jnp.stack(sent[2]), across[1], found)))
    found = score(2, [score(1, [found])])
    mine = merge([found[0]] + [swap_hi(found[step], step) for step in range(1, tall)])
    return merge([mine] + [swap_part(mine, step) for step in range(1, parts)])


def local(hidden, gain, head, target_ids, seq_lens, seq_owner):
    groups = lax.axis_size("dp")
    slots, features = hidden.shape
    owners = jnp.arange(groups, dtype=jnp.int32)
    loads = jnp.sum(jnp.where(seq_owner[:, None] == owners[None, :], seq_lens[:, None], 0), axis=0).astype(jnp.int32)
    fits = (
        (groups, lax.axis_size("vocab")) == (8, 4)
        and slots % ROWS == 0
        and slots // ROWS <= TILE
        and 2 * ROWS <= features
        and head.shape[1] % (groups // 2 * TILE) == 0
    )
    transport = by_axes if fits else by_collectives
    scores = transport(hidden, gain.astype(jnp.float32)[None], head, target_ids, seq_lens, seq_owner)
    top, total, weighted, picked = (scores[index] for index in range(4))
    spread = jnp.log(total)
    logprob = picked - (top + spread)
    entropy = spread - weighted / total
    live = jnp.arange(slots, dtype=jnp.int32) < loads[lax.axis_index("dp")]
    return (jnp.where(live, logprob, 0.0), jnp.where(live, entropy, 0.0))


def solution(mesh):
    return jax.shard_map(
        local,
        mesh=mesh,
        in_specs=(P("dp", "vocab"), P(), P("dp", "vocab"), P("dp"), P(), P()),
        out_specs=(P("dp"), P("dp")),
        check_vma=False,
    )
```

```python
import functools

import jax
import jax.numpy as jnp
from jax import lax
from jax.experimental import pallas as pl
from jax.experimental.pallas import tpu as pltpu
from jax.sharding import PartitionSpec as P

EPS = 1e-05
LOW = -3.0e38
LANES = 128
TILE = 16
PIECES = (8, 7, 5)
ROWS = 256
TOKEN_BYTES = 17 * 2**20


def assemble_kernel(near_first, gain_ref, *refs):
    target = refs[-1]
    sources = []
    for away, ref in enumerate(refs[:-1]):
        for index in range(ref.shape[0]):
            part = lax.axis_index("vocab") ^ (2 * index + away) if near_first else index
            sources.append((ref, index, part))
    features = refs[0].shape[3]
    for start in range(0, target.shape[3], LANES):
        lanes = slice(start, start + LANES)
        square = sum(
            jnp.sum(jnp.square(ref[at, 0, lanes].astype(jnp.float32)), axis=1, keepdims=True) for ref, at, _ in sources
        )
        scale = lax.rsqrt(square / (features * len(sources)) + EPS)
        for ref, at, part in sources:
            first = pl.multiple_of(part * features, features)
            value = ref[at, 0, lanes].astype(jnp.float32) * scale * gain_ref[:, pl.ds(first, features)]
            target[0, 0, pl.ds(first, features), lanes] = value.T.astype(target.dtype)


def assemble(gain, sources, rows):
    _, count, slots, features = sources[0].shape
    splits = slots // rows
    wide = features * sum(y.shape[0] for y in sources)
    return pl.pallas_call(
        functools.partial(assemble_kernel, len(sources) > 1),
        grid=(count, splits),
        in_specs=[pl.BlockSpec((1, wide), lambda i, j: (0, 0))]
        + [pl.BlockSpec((y.shape[0], 1, rows, features), lambda i, j: (0, i, j, 0)) for y in sources],
        out_specs=pl.BlockSpec((1, 1, wide, rows), lambda i, j: (i, j, 0, 0)),
        out_shape=jax.ShapeDtypeStruct((count, splits, wide, rows), sources[0].dtype),
        compiler_params=pltpu.CompilerParams(vmem_limit_bytes=24 * 2**20),
        cost_estimate=pl.CostEstimate(
            flops=6 * count * splits * rows * wide,
            bytes_accessed=4 * count * splits * rows * wide,
            transcendentals=count * splits * rows,
        ),
    )(gain, *sources)


def stats_kernel(plan, counts, start_ref, lens_ref, owner_ref, *refs):
    out_ref, head, held, logits, ids, order, sems, token_sems = refs[-8:]
    members = []
    for count in counts:
        members.append(refs[:count])
        refs = refs[count:]
    token_refs, id_refs, head_refs, before = members
    splits, _, rows = token_refs[0].shape[1:]
    groups = len(token_refs) * token_refs[0].shape[0]
    width, depth = head.shape[0], head_refs[0].shape[-1]
    real, base = plan.columns()

    copies = []
    for source, group in plan.head_parts(head_refs):
        lane = pl.multiple_of(group * depth, LANES)
        copies.append(pltpu.make_async_copy(source, head.at[:, pl.ds(lane, depth)], sems.at[len(copies)]))
    for copy in copies:
        copy.start()

    def one_group(group, live):
        def one_sequence(index, load):
            return load + jnp.where(owner_ref[index] == plan.group(group), lens_ref[index], 0)

        load = lax.fori_loop(0, lens_ref.shape[0], one_sequence, jnp.int32(0))
        for split in range(splits):
            order[live] = group * splits + split
            live = live + jnp.where(start_ref[0] + split * rows < load, 1, 0)
        return live

    live = lax.fori_loop(0, groups, one_group, jnp.int32(0))

    def fetch(step, slot):
        group, split = order[step] // splits, order[step] % splits
        each = token_refs[0].shape[0]
        for index, source in enumerate(token_refs):

            @pl.when(group // each == index)
            def _():
                pltpu.make_async_copy(source.at[group % each, split], held.at[slot], token_sems.at[slot]).start()

    @pl.when(live > 0)
    def _():
        fetch(0, 0)

    out_ref[...] = jnp.zeros_like(out_ref)
    for index, source in enumerate(id_refs):
        places = source[...] - base
        ids[pl.ds(index * source.shape[0], source.shape[0])] = jnp.where(places < real, places, -1)
    for copy in copies:
        copy.wait()

    def body(step, carry):
        slot = lax.rem(step, 2)
        pltpu.make_async_copy(token_refs[0].at[0, 0], held.at[slot], token_sems.at[slot]).wait()

        @pl.when(step + 1 < live)
        def _():
            fetch(step + 1, 1 - slot)

        logits[...] = jnp.dot(head[...], held[slot], preferred_element_type=jnp.float32)

        @pl.when(real < width)
        def _():
            column = lax.broadcasted_iota(jnp.int32, (width - plan.least, rows), 0) + plan.least
            logits[plan.least :] = jnp.where(column < real, logits[plan.least :], LOW)

        block = order[step]
        target = plan.slot(block // splits)
        split = block % splits
        column = lax.broadcasted_iota(jnp.int32, (width, LANES), 0)
        for start in range(0, rows, LANES):
            lanes = slice(start, start + LANES)
            values = logits[:, lanes]
            top = jnp.max(values, axis=0, keepdims=True)
            shifted = jnp.maximum(values - top, -1.0e4)
            expo = jnp.exp(shifted)
            total = jnp.sum(expo, axis=0, keepdims=True)
            weighted = jnp.sum(expo * shifted, axis=0, keepdims=True)
            picked = jnp.sum(jnp.where(column == ids[block, :, lanes], values, 0.0), axis=0, keepdims=True)
            place = pl.ds(pl.multiple_of(split * rows + start, LANES), LANES)
            if before:
                top, total, weighted, picked = joined(
                    [(top, total, weighted, picked), [before[0][target, index : index + 1, place] for index in range(4)]]
                )
            for index, member in enumerate((top, total, weighted, picked)):
                out_ref[target, index : index + 1, place] = member
        return carry

    lax.fori_loop(0, live, body, 0)


def stats(plan, start, seq_lens, seq_owner, tokens, ids, heads, before):
    groups, splits, wide, rows = tokens[0].shape
    groups *= len(tokens)
    width = plan.width
    smem = pl.BlockSpec(memory_space=pltpu.SMEM)
    vmem = pl.BlockSpec(memory_space=pltpu.VMEM)
    anywhere = pl.BlockSpec(memory_space=pl.ANY)
    return pl.pallas_call(
        functools.partial(stats_kernel, plan, (len(tokens), len(ids), len(heads), len(before))),
        in_specs=[smem] * 3
        + [anywhere] * len(tokens)
        + [vmem] * len(ids)
        + [anywhere] * len(heads)
        + [vmem] * len(before),
        out_specs=vmem,
        scratch_shapes=[
            pltpu.VMEM((width, wide), jnp.bfloat16),
            pltpu.VMEM((2, wide, rows), jnp.bfloat16),
            pltpu.VMEM((width, rows), jnp.float32),
            pltpu.VMEM((groups * splits, 1, rows), jnp.int32),
            pltpu.SMEM((groups * splits + 1,), jnp.int32),
            pltpu.SemaphoreType.DMA((wide // heads[0].shape[-1],)),
            pltpu.SemaphoreType.DMA((2,)),
        ],
        out_shape=jax.ShapeDtypeStruct((groups, 4, splits * rows), jnp.float32),
        compiler_params=pltpu.CompilerParams(vmem_limit_bytes=24 * 2**20),
        cost_estimate=pl.CostEstimate(
            flops=groups * splits * rows * wide * width // 8,
            bytes_accessed=wide * width,
            transcendentals=groups * splits * rows * width // 8,
        ),
    )(start, seq_lens, seq_owner, *tokens, *ids, *heads, *before)


class Spread:
    def __init__(self, breadth, groups):
        self.breadth = breadth
        self.cuts = [breadth * index // groups // TILE * TILE for index in range(groups)] + [breadth]
        sizes = [end - start for start, end in zip(self.cuts, self.cuts[1:])]
        self.width, self.least = max(sizes), min(sizes)

    def spread(self, turned):
        turned = jnp.pad(turned, ((0, self.cuts[-2] + self.width - self.breadth), (0, 0)))
        return jnp.stack([turned[start : start + self.width] for start in self.cuts[:-1]])

    def columns(self):
        position = lax.axis_index("dp")
        start, end = 0, self.breadth
        for index, (first, last) in enumerate(zip(self.cuts, self.cuts[1:])):
            start = jnp.where(position == index, first, start)
            end = jnp.where(position == index, last, end)
        return end - start, lax.axis_index("vocab") * self.breadth + start

    def head_parts(self, refs):
        return [(refs[0], 0)]

    def group(self, group):
        return group

    def slot(self, group):
        return group


class Line:
    def __init__(self, breadth, chunk, start, width):
        self.breadth, self.chunk, self.start = breadth, chunk, start
        self.width = self.least = width

    def columns(self):
        hi = lax.axis_index("dp") // 2
        return self.width, lax.axis_index("vocab") * self.breadth + hi * self.chunk + self.start

    def head_parts(self, refs):
        position = lax.axis_index("dp")
        hi, low = position // 2, position % 2
        here = pl.ds(self.start, self.width)
        mine = [refs[0].at[hi, here], *refs[2:5]]
        other = [refs[1].at[here], *(refs[5].at[index] for index in range(3))]
        found = [(source, 2 * (hi ^ step) + low) for step, source in enumerate(mine)]
        return found + [(source, 2 * (hi ^ step) + (low ^ 1)) for step, source in enumerate(other)]

    def slot(self, group):
        hi = lax.axis_index("dp") // 2
        middle = (hi == 1) | (hi == 2)
        return jnp.where(middle & (group >= 2), 5 - group, group)

    def group(self, group):
        position = lax.axis_index("dp")
        return 2 * (position // 2 ^ self.slot(group)) + position % 2


def after(x, *others):
    return lax.optimization_barrier((x, *others))[0]


def joined(members):
    best = functools.reduce(jnp.maximum, [top for top, _, _, _ in members])
    total = weighted = picked = 0.0
    for top, other_total, other_weighted, other_picked in members:
        shift = jnp.maximum(top - best, -1.0e4)
        factor = jnp.exp(shift)
        total += other_total * factor
        weighted += factor * (other_weighted + other_total * shift)
        picked += other_picked
    return best, total, weighted, picked


def merge(members):
    return jnp.stack(joined([[member[..., index, :] for index in range(4)] for member in members]), axis=-2)


def by_collectives(hidden, gain, head, target_ids, seq_lens, seq_owner):
    groups = lax.axis_size("dp")
    parts = lax.axis_size("vocab")
    slots, features = hidden.shape
    depth, breadth = head.shape
    plan = Spread(breadth, groups)
    ids = lax.all_gather(target_ids, "dp", axis=0)

    columns = lax.all_to_all(plan.spread(head.T), "dp", split_axis=0, concat_axis=0, tiled=True)
    columns = columns.transpose(1, 0, 2).reshape(plan.width, groups * depth)

    splits = -(-groups * slots * features * parts * 2 // TOKEN_BYTES)
    while slots % splits or (slots // splits) % LANES:
        splits += 1
    rows = slots // splits

    def score(start):
        piece = lax.dynamic_slice_in_dim(hidden, start, rows)
        x = lax.all_gather(piece, ("vocab", "dp"), axis=0).reshape(parts, groups, rows, features)
        x = assemble(gain, [x], rows)
        wanted = lax.dynamic_slice_in_dim(ids, start, rows, axis=1)[:, None]
        return stats(plan, start[None], seq_lens, seq_owner, [x], [wanted], [columns], [])

    found = lax.map(score, jnp.arange(splits, dtype=jnp.int32) * rows)
    found = found.transpose(1, 2, 0, 3).reshape(groups, 4, slots)
    found = lax.all_to_all(found, "dp", split_axis=0, concat_axis=0, tiled=True)
    mine = lax.all_gather(merge(list(found)), "vocab", axis=0)
    return merge(list(mine))


def by_axes(hidden, gain, head, target_ids, seq_lens, seq_owner):
    groups = lax.axis_size("dp")
    parts = lax.axis_size("vocab")
    tall = groups // 2
    hi = lax.axis_index("dp") // 2
    slots, features = hidden.shape
    depth, breadth = head.shape
    splits = slots // ROWS
    middle = (hi == 1) | (hi == 2)
    chunk = breadth // tall
    ends = [chunk * sum(PIECES[:n]) // sum(PIECES) // TILE * TILE for n in range(len(PIECES))] + [chunk]
    cuts = [(start, end - start) for start, end in zip(ends, ends[1:])]

    def swap_hi(x, step):
        return lax.ppermute(x, "dp", [(g, g ^ (2 * step)) for g in range(groups)])

    def swap_lo(x):
        return lax.ppermute(x, "dp", [(g, g ^ 1) for g in range(groups)])

    def swap_part(x, step):
        return lax.ppermute(x, "vocab", [(v, v ^ step) for v in range(parts)])

    def along(x, moves):
        return lax.ppermute(x, "dp", [(2 * a + side, 2 * b + side) for a, b in moves for side in range(2)])

    code = jnp.stack([target_ids >> 8, target_ids & 255]).astype(hidden.dtype).reshape(2, splits, ROWS)
    code = code.transpose(1, 0, 2).reshape(splits, 2 * ROWS)
    own = jnp.concatenate([hidden, jnp.pad(code, ((0, TILE - splits), (0, features - 2 * ROWS)))])
    near = swap_hi(own, 1)
    cross = along(own, [(1, 2), (2, 1)])
    cross_near = along(near, [(1, 2), (2, 1)])
    out = along(cross, [(1, 0), (2, 3)])
    out_near = along(cross_near, [(1, 0), (2, 3)])

    turned = head.T.reshape(tall, chunk, depth)

    def block(step, start, width):
        return lax.dynamic_slice(turned, (hi ^ step, start, 0), (1, width, depth))[0]

    blocks = [[block(step, *cut) for step in (1, 2, 3)] for cut in cuts]

    def to_hi(piece, *others):
        return [swap_hi(after(y, *others), step) for step, y in enumerate(blocks[piece], 1)]

    def over_x(x):
        return swap_part(x, 2)

    def both(x, y, x_across, y_across):
        return jnp.stack([jnp.stack([x, y]), jnp.stack([x_across, y_across])])

    def ready(half, whole):
        code = half[0, :, slots : slots + splits, : 2 * ROWS].astype(jnp.int32).reshape(2 * splits, 2, ROWS)
        return assemble(gain, [half, whole], ROWS), code[:, :1] * 256 + code[:, 1:]

    def score(piece, before):
        start, width = cuts[piece]
        plan = Line(breadth, chunk, start, width)
        heads = [turned, local_block, *sent[piece], across[piece]]
        return stats(plan, jnp.zeros(1, jnp.int32), seq_lens, seq_owner, tokens, ids, heads, before)

    local_block = swap_lo(block(0, 0, chunk))
    own_across = over_x(own)
    near_across = over_x(after(near, own_across, local_block))
    sent = [to_hi(0, out, cross_near, near_across, *blocks[1], *blocks[2])]
    far = jnp.where(middle, cross, out)
    far_across = over_x(far)
    last = jnp.where(middle, cross_near, out_near)
    last_across = over_x(after(last, *sent[0]))
    sent.append(to_hi(1, *sent[0], far_across))
    front_half = both(own, near, own_across, near_across)
    front_whole = swap_part(front_half, 1)
    back_half = both(far, last, far_across, last_across)
    back_whole = swap_part(after(back_half, *sent[1]), 1)
    tokens, ids = zip(ready(front_half, front_whole), ready(back_half, back_whole))
    sent.append(to_hi(2, *sent[1], tokens[0]))
    across = [swap_lo(jnp.stack(sent[0]))]
    across.append(swap_lo(jnp.stack(sent[1])))
    found = score(0, [])
    across.append(swap_lo(after(jnp.stack(sent[2]), across[1], found)))
    found = score(2, [score(1, [found])])
    mine = merge([found[0]] + [swap_hi(found[step], step) for step in range(1, tall)])
    return merge([mine] + [swap_part(mine, step) for step in range(1, parts)])


def local(hidden, gain, head, target_ids, seq_lens, seq_owner):
    groups = lax.axis_size("dp")
    slots, features = hidden.shape
    owners = jnp.arange(groups, dtype=jnp.int32)
    loads = jnp.sum(jnp.where(seq_owner[:, None] == owners[None, :], seq_lens[:, None], 0), axis=0).astype(jnp.int32)
    fits = (
        (groups, lax.axis_size("vocab")) == (8, 4)
        and slots % ROWS == 0
        and slots // ROWS <= TILE
        and 2 * ROWS <= features
        and head.shape[1] % (groups // 2 * TILE) == 0
    )
    transport = by_axes if fits else by_collectives
    scores = transport(hidden, gain.astype(jnp.float32)[None], head, target_ids, seq_lens, seq_owner)
    top, total, weighted, picked = (scores[index] for index in range(4))
    spread = jnp.log(total)
    logprob = picked - (top + spread)
    entropy = spread - weighted / total
    live = jnp.arange(slots, dtype=jnp.int32) < loads[lax.axis_index("dp")]
    return (jnp.where(live, logprob, 0.0), jnp.where(live, entropy, 0.0))


def solution(mesh):
    return jax.shard_map(
        local,
        mesh=mesh,
        in_specs=(P("dp", "vocab"), P(), P("dp", "vocab"), P("dp"), P(), P()),
        out_specs=(P("dp"), P("dp")),
        check_vma=False,
    )
```

```python
import functools

import jax
import jax.numpy as jnp
from jax import lax
from jax.experimental import pallas as pl
from jax.experimental.pallas import tpu as pltpu
from jax.sharding import PartitionSpec as P

EPS = 1e-05
LOW = -3.0e38
LANES = 128
TILE = 16
PIECES = (8, 7, 5)
ROWS = 256
TOKEN_BYTES = 17 * 2**20


def assemble_kernel(near_first, gain_ref, *refs):
    target = refs[-1]
    sources = []
    for away, ref in enumerate(refs[:-1]):
        for index in range(ref.shape[0]):
            part = lax.axis_index("vocab") ^ (2 * index + away) if near_first else index
            sources.append((ref, index, part))
    features = refs[0].shape[3]
    for start in range(0, target.shape[3], LANES):
        lanes = slice(start, start + LANES)
        square = sum(
            jnp.sum(jnp.square(ref[at, 0, lanes].astype(jnp.float32)), axis=1, keepdims=True) for ref, at, _ in sources
        )
        scale = lax.rsqrt(square / (features * len(sources)) + EPS)
        for ref, at, part in sources:
            first = pl.multiple_of(part * features, features)
            value = ref[at, 0, lanes].astype(jnp.float32) * scale * gain_ref[:, pl.ds(first, features)]
            target[0, 0, pl.ds(first, features), lanes] = value.T.astype(target.dtype)


def assemble(gain, sources, rows):
    _, count, slots, features = sources[0].shape
    splits = slots // rows
    wide = features * sum(y.shape[0] for y in sources)
    return pl.pallas_call(
        functools.partial(assemble_kernel, len(sources) > 1),
        grid=(count, splits),
        in_specs=[pl.BlockSpec((1, wide), lambda i, j: (0, 0))]
        + [pl.BlockSpec((y.shape[0], 1, rows, features), lambda i, j: (0, i, j, 0)) for y in sources],
        out_specs=pl.BlockSpec((1, 1, wide, rows), lambda i, j: (i, j, 0, 0)),
        out_shape=jax.ShapeDtypeStruct((count, splits, wide, rows), sources[0].dtype),
        compiler_params=pltpu.CompilerParams(vmem_limit_bytes=24 * 2**20),
        cost_estimate=pl.CostEstimate(
            flops=6 * count * splits * rows * wide,
            bytes_accessed=4 * count * splits * rows * wide,
            transcendentals=count * splits * rows,
        ),
    )(gain, *sources)


def stats_kernel(plan, counts, start_ref, lens_ref, owner_ref, *refs):
    out_ref, head, held, logits, ids, order, sems, token_sems = refs[-8:]
    members = []
    for count in counts:
        members.append(refs[:count])
        refs = refs[count:]
    token_refs, id_refs, head_refs, before = members
    splits, _, rows = token_refs[0].shape[1:]
    groups = len(token_refs) * token_refs[0].shape[0]
    width, depth = head.shape[0], head_refs[0].shape[-1]
    real, base = plan.columns()

    copies = []
    for source, first, group in plan.head_parts(head_refs):
        target = head.at[pl.ds(first, source.shape[0]), pl.ds(pl.multiple_of(group * depth, LANES), depth)]
        copies.append(pltpu.make_async_copy(source, target, sems.at[len(copies)]))
    for copy in copies:
        copy.start()

    def one_group(group, live):
        def one_sequence(index, load):
            return load + jnp.where(owner_ref[index] == plan.group(group), lens_ref[index], 0)

        load = lax.fori_loop(0, lens_ref.shape[0], one_sequence, jnp.int32(0))
        for split in range(splits):
            order[live] = group * splits + split
            live = live + jnp.where(start_ref[0] + split * rows < load, 1, 0)
        return live

    live = lax.fori_loop(0, groups, one_group, jnp.int32(0))

    def fetch(step, slot):
        group, split = order[step] // splits, order[step] % splits
        each = token_refs[0].shape[0]
        for index, source in enumerate(token_refs):

            @pl.when(group // each == index)
            def _():
                pltpu.make_async_copy(source.at[group % each, split], held.at[slot], token_sems.at[slot]).start()

    @pl.when(live > 0)
    def _():
        fetch(0, 0)

    out_ref[...] = jnp.zeros_like(out_ref)
    for index, source in enumerate(id_refs):
        places = source[...] - base
        ids[pl.ds(index * source.shape[0], source.shape[0])] = jnp.where(places < real, places, -1)
    for copy in copies:
        copy.wait()

    def body(step, carry):
        slot = lax.rem(step, 2)
        pltpu.make_async_copy(token_refs[0].at[0, 0], held.at[slot], token_sems.at[slot]).wait()

        @pl.when(step + 1 < live)
        def _():
            fetch(step + 1, 1 - slot)

        logits[...] = jnp.dot(head[...], held[slot], preferred_element_type=jnp.float32)

        @pl.when(real < width)
        def _():
            column = lax.broadcasted_iota(jnp.int32, (width - plan.least, rows), 0) + plan.least
            logits[plan.least :] = jnp.where(column < real, logits[plan.least :], LOW)

        block = order[step]
        target = plan.slot(block // splits)
        split = block % splits
        column = lax.broadcasted_iota(jnp.int32, (width, LANES), 0)
        for start in range(0, rows, LANES):
            lanes = slice(start, start + LANES)
            values = logits[:, lanes]
            top = jnp.max(values, axis=0, keepdims=True)
            shifted = jnp.maximum(values - top, -1.0e4)
            expo = jnp.exp(shifted)
            total = jnp.sum(expo, axis=0, keepdims=True)
            weighted = jnp.sum(expo * shifted, axis=0, keepdims=True)
            picked = jnp.sum(jnp.where(column == ids[block, :, lanes], values, 0.0), axis=0, keepdims=True)
            place = pl.ds(pl.multiple_of(split * rows + start, LANES), LANES)
            if before:
                top, total, weighted, picked = joined(
                    [(top, total, weighted, picked), [before[0][target, index : index + 1, place] for index in range(4)]]
                )
            for index, member in enumerate((top, total, weighted, picked)):
                out_ref[target, index : index + 1, place] = member
        return carry

    lax.fori_loop(0, live, body, 0)


def stats(plan, start, seq_lens, seq_owner, tokens, ids, heads, before):
    groups, splits, wide, rows = tokens[0].shape
    groups *= len(tokens)
    width = plan.width
    smem = pl.BlockSpec(memory_space=pltpu.SMEM)
    vmem = pl.BlockSpec(memory_space=pltpu.VMEM)
    anywhere = pl.BlockSpec(memory_space=pltpu.HBM)
    return pl.pallas_call(
        functools.partial(stats_kernel, plan, (len(tokens), len(ids), len(heads), len(before))),
        in_specs=[smem] * 3
        + [anywhere] * len(tokens)
        + [vmem] * len(ids)
        + [anywhere] * len(heads)
        + [vmem] * len(before),
        out_specs=vmem,
        scratch_shapes=[
            pltpu.VMEM((width, wide), jnp.bfloat16),
            pltpu.VMEM((2, wide, rows), jnp.bfloat16),
            pltpu.VMEM((width, rows), jnp.float32),
            pltpu.VMEM((groups * splits, 1, rows), jnp.int32),
            pltpu.SMEM((groups * splits + 1,), jnp.int32),
            pltpu.SemaphoreType.DMA((plan.copies,)),
            pltpu.SemaphoreType.DMA((2,)),
        ],
        out_shape=jax.ShapeDtypeStruct((groups, 4, splits * rows), jnp.float32),
        compiler_params=pltpu.CompilerParams(vmem_limit_bytes=32 * 2**20),
        cost_estimate=pl.CostEstimate(
            flops=groups * splits * rows * wide * width // 8,
            bytes_accessed=wide * width,
            transcendentals=groups * splits * rows * width // 8,
        ),
    )(start, seq_lens, seq_owner, *tokens, *ids, *heads, *before)


class Spread:
    def __init__(self, breadth, groups):
        self.breadth = breadth
        self.cuts = [breadth * index // groups // TILE * TILE for index in range(groups)] + [breadth]
        sizes = [end - start for start, end in zip(self.cuts, self.cuts[1:])]
        self.width, self.least = max(sizes), min(sizes)
        self.copies = 1

    def spread(self, turned):
        turned = jnp.pad(turned, ((0, self.cuts[-2] + self.width - self.breadth), (0, 0)))
        return jnp.stack([turned[start : start + self.width] for start in self.cuts[:-1]])

    def columns(self):
        position = lax.axis_index("dp")
        start, end = 0, self.breadth
        for index, (first, last) in enumerate(zip(self.cuts, self.cuts[1:])):
            start = jnp.where(position == index, first, start)
            end = jnp.where(position == index, last, end)
        return end - start, lax.axis_index("vocab") * self.breadth + start

    def head_parts(self, refs):
        return [(refs[0], 0, 0)]

    def group(self, group):
        return group

    def slot(self, group):
        return group


class Line:
    def __init__(self, breadth, chunk, cuts):
        self.breadth, self.chunk, self.cuts = breadth, chunk, cuts
        self.start = cuts[0][0]
        self.width = self.least = sum(width for _, width in cuts)
        self.copies = 2 + 6 * len(cuts)

    def columns(self):
        hi = lax.axis_index("dp") // 2
        return self.width, lax.axis_index("vocab") * self.breadth + hi * self.chunk + self.start

    def head_parts(self, refs):
        position = lax.axis_index("dp")
        hi, low = position // 2, position % 2
        here = pl.ds(self.start, self.width)
        found = [(refs[0].at[hi, here], 0, 2 * hi + low), (refs[1].at[here], 0, 2 * hi + (low ^ 1))]
        for index, (start, _) in enumerate(self.cuts):
            *mine, other = refs[2 + 4 * index : 6 + 4 * index]
            for step in (1, 2, 3):
                found.append((mine[step - 1], start - self.start, 2 * (hi ^ step) + low))
                found.append((other.at[step - 1], start - self.start, 2 * (hi ^ step) + (low ^ 1)))
        return found

    def slot(self, group):
        hi = lax.axis_index("dp") // 2
        middle = (hi == 1) | (hi == 2)
        return jnp.where(middle & (group >= 2), 5 - group, group)

    def group(self, group):
        position = lax.axis_index("dp")
        return 2 * (position // 2 ^ self.slot(group)) + position % 2


def after(x, *others):
    return lax.optimization_barrier((x, *others))[0]


def joined(members):
    best = functools.reduce(jnp.maximum, [top for top, _, _, _ in members])
    total = weighted = picked = 0.0
    for top, other_total, other_weighted, other_picked in members:
        shift = jnp.maximum(top - best, -1.0e4)
        factor = jnp.exp(shift)
        total += other_total * factor
        weighted += factor * (other_weighted + other_total * shift)
        picked += other_picked
    return best, total, weighted, picked


def merge(members):
    return jnp.stack(joined([[member[..., index, :] for index in range(4)] for member in members]), axis=-2)


def by_collectives(hidden, gain, head, target_ids, seq_lens, seq_owner):
    groups = lax.axis_size("dp")
    parts = lax.axis_size("vocab")
    slots, features = hidden.shape
    depth, breadth = head.shape
    plan = Spread(breadth, groups)
    ids = lax.all_gather(target_ids, "dp", axis=0)

    columns = lax.all_to_all(plan.spread(head.T), "dp", split_axis=0, concat_axis=0, tiled=True)
    columns = columns.transpose(1, 0, 2).reshape(plan.width, groups * depth)

    splits = -(-groups * slots * features * parts * 2 // TOKEN_BYTES)
    while slots % splits or (slots // splits) % LANES:
        splits += 1
    rows = slots // splits

    def score(start):
        piece = lax.dynamic_slice_in_dim(hidden, start, rows)
        x = lax.all_gather(piece, ("vocab", "dp"), axis=0).reshape(parts, groups, rows, features)
        x = assemble(gain, [x], rows)
        wanted = lax.dynamic_slice_in_dim(ids, start, rows, axis=1)[:, None]
        return stats(plan, start[None], seq_lens, seq_owner, [x], [wanted], [columns], [])

    found = lax.map(score, jnp.arange(splits, dtype=jnp.int32) * rows)
    found = found.transpose(1, 2, 0, 3).reshape(groups, 4, slots)
    found = lax.all_to_all(found, "dp", split_axis=0, concat_axis=0, tiled=True)
    mine = lax.all_gather(merge(list(found)), "vocab", axis=0)
    return merge(list(mine))


def by_axes(hidden, gain, head, target_ids, seq_lens, seq_owner):
    groups = lax.axis_size("dp")
    parts = lax.axis_size("vocab")
    tall = groups // 2
    hi = lax.axis_index("dp") // 2
    slots, features = hidden.shape
    depth, breadth = head.shape
    splits = slots // ROWS
    middle = (hi == 1) | (hi == 2)
    chunk = breadth // tall
    ends = [chunk * sum(PIECES[:n]) // sum(PIECES) // TILE * TILE for n in range(len(PIECES))] + [chunk]
    cuts = [(start, end - start) for start, end in zip(ends, ends[1:])]

    def swap_hi(x, step):
        return lax.ppermute(x, "dp", [(g, g ^ (2 * step)) for g in range(groups)])

    def swap_lo(x):
        return lax.ppermute(x, "dp", [(g, g ^ 1) for g in range(groups)])

    def swap_part(x, step):
        return lax.ppermute(x, "vocab", [(v, v ^ step) for v in range(parts)])

    def along(x, moves):
        return lax.ppermute(x, "dp", [(2 * a + side, 2 * b + side) for a, b in moves for side in range(2)])

    code = jnp.stack([target_ids >> 8, target_ids & 255]).astype(hidden.dtype).reshape(2, splits, ROWS)
    code = code.transpose(1, 0, 2).reshape(splits, 2 * ROWS)
    own = jnp.concatenate([hidden, jnp.pad(code, ((0, TILE - splits), (0, features - 2 * ROWS)))])
    near = swap_hi(own, 1)
    cross = along(own, [(1, 2), (2, 1)])
    cross_near = along(near, [(1, 2), (2, 1)])
    out = along(cross, [(1, 0), (2, 3)])
    out_near = along(cross_near, [(1, 0), (2, 3)])

    turned = head.T.reshape(tall, chunk, depth)

    def block(step, start, width):
        return lax.dynamic_slice(turned, (hi ^ step, start, 0), (1, width, depth))[0]

    blocks = [[block(step, *cut) for step in (1, 2, 3)] for cut in cuts]

    def to_hi(piece, *others):
        return [swap_hi(after(y, *others), step) for step, y in enumerate(blocks[piece], 1)]

    def over_x(x):
        return swap_part(x, 2)

    def both(x, y, x_across, y_across):
        return jnp.stack([jnp.stack([x, y]), jnp.stack([x_across, y_across])])

    def ready(half, whole):
        code = half[0, :, slots : slots + splits, : 2 * ROWS].astype(jnp.int32).reshape(2 * splits, 2, ROWS)
        return assemble(gain, [half, whole], ROWS), code[:, :1] * 256 + code[:, 1:]

    def score(pieces, before):
        plan = Line(breadth, chunk, [cuts[piece] for piece in pieces])
        heads = [turned, local_block, *(y for piece in pieces for y in (*sent[piece], across[piece]))]
        return stats(plan, jnp.zeros(1, jnp.int32), seq_lens, seq_owner, tokens, ids, heads, before)

    local_block = swap_lo(block(0, 0, chunk))
    own_across = over_x(own)
    near_across = over_x(after(near, cross, own_across, local_block))
    sent = [to_hi(0, out, cross_near, near_across, *blocks[1], *blocks[2])]
    far = jnp.where(middle, cross, out)
    far_across = over_x(far)
    last = jnp.where(middle, cross_near, out_near)
    last_across = over_x(after(last, *sent[0]))
    sent.append(to_hi(1, *sent[0], far_across))
    front_half = both(own, near, own_across, near_across)
    across = [swap_lo(jnp.stack(sent[0]))]
    front = ready(front_half, swap_part(after(front_half, *sent[1], across[0]), 1))
    back_half = both(far, last, far_across, last_across)
    back = ready(back_half, swap_part(after(back_half, *sent[1], across[0]), 1))
    tokens, ids = zip(front, back)
    sent.append(to_hi(2, *sent[1]))
    across.append(swap_lo(jnp.stack(sent[1])))
    across.append(swap_lo(after(jnp.stack(sent[2]), across[1])))
    found = score((2,), [score((0, 1), [])])
    mine = merge([found[0]] + [swap_hi(found[step], step) for step in range(1, tall)])
    return merge([mine] + [swap_part(mine, step) for step in range(1, parts)])


def local(hidden, gain, head, target_ids, seq_lens, seq_owner):
    groups = lax.axis_size("dp")
    slots, features = hidden.shape
    owners = jnp.arange(groups, dtype=jnp.int32)
    loads = jnp.sum(jnp.where(seq_owner[:, None] == owners[None, :], seq_lens[:, None], 0), axis=0).astype(jnp.int32)
    fits = (
        (groups, lax.axis_size("vocab")) == (8, 4)
        and slots % ROWS == 0
        and slots // ROWS <= TILE
        and 2 * ROWS <= features
        and head.shape[1] % (groups // 2 * TILE) == 0
    )
    transport = by_axes if fits else by_collectives
    scores = transport(hidden, gain.astype(jnp.float32)[None], head, target_ids, seq_lens, seq_owner)
    top, total, weighted, picked = (scores[index] for index in range(4))
    spread = jnp.log(total)
    logprob = picked - (top + spread)
    entropy = spread - weighted / total
    live = jnp.arange(slots, dtype=jnp.int32) < loads[lax.axis_index("dp")]
    return (jnp.where(live, logprob, 0.0), jnp.where(live, entropy, 0.0))


def solution(mesh):
    return jax.shard_map(
        local,
        mesh=mesh,
        in_specs=(P("dp", "vocab"), P(), P("dp", "vocab"), P("dp"), P(), P()),
        out_specs=(P("dp"), P("dp")),
        check_vma=False,
    )
```

```python
import functools

import jax
import jax.numpy as jnp
from jax import lax
from jax.experimental import pallas as pl
from jax.experimental.pallas import tpu as pltpu
from jax.sharding import PartitionSpec as P

EPS = 1e-05
LOW = -3.0e38
LANES = 128
TILE = 16
PIECES = (8, 7, 5)
ROWS = 256
TOKEN_BYTES = 17 * 2**20


def assemble_kernel(near_first, gain_ref, *refs):
    target = refs[-1]
    sources = []
    for away, ref in enumerate(refs[:-1]):
        for index in range(ref.shape[0]):
            part = lax.axis_index("vocab") ^ (2 * index + away) if near_first else index
            sources.append((ref, index, part))
    features = refs[0].shape[3]
    for start in range(0, target.shape[3], LANES):
        lanes = slice(start, start + LANES)
        square = sum(
            jnp.sum(jnp.square(ref[at, 0, lanes].astype(jnp.float32)), axis=1, keepdims=True) for ref, at, _ in sources
        )
        scale = lax.rsqrt(square / (features * len(sources)) + EPS)
        for ref, at, part in sources:
            first = pl.multiple_of(part * features, features)
            value = ref[at, 0, lanes].astype(jnp.float32) * scale * gain_ref[:, pl.ds(first, features)]
            target[0, 0, pl.ds(first, features), lanes] = value.T.astype(target.dtype)


def assemble(gain, sources, rows):
    _, count, slots, features = sources[0].shape
    splits = slots // rows
    wide = features * sum(y.shape[0] for y in sources)
    return pl.pallas_call(
        functools.partial(assemble_kernel, len(sources) > 1),
        grid=(count, splits),
        in_specs=[pl.BlockSpec((1, wide), lambda i, j: (0, 0))]
        + [pl.BlockSpec((y.shape[0], 1, rows, features), lambda i, j: (0, i, j, 0)) for y in sources],
        out_specs=pl.BlockSpec((1, 1, wide, rows), lambda i, j: (i, j, 0, 0)),
        out_shape=jax.ShapeDtypeStruct((count, splits, wide, rows), sources[0].dtype),
        compiler_params=pltpu.CompilerParams(vmem_limit_bytes=60 * 2**20),
        cost_estimate=pl.CostEstimate(
            flops=6 * count * splits * rows * wide,
            bytes_accessed=4 * count * splits * rows * wide,
            transcendentals=count * splits * rows,
        ),
    )(gain, *sources)


def stats_kernel(plan, counts, start_ref, lens_ref, owner_ref, *refs):
    out_ref, head, held, logits, ids, order, sems, token_sems = refs[-8:]
    members = []
    for count in counts:
        members.append(refs[:count])
        refs = refs[count:]
    token_refs, id_refs, head_refs, before = members
    splits, _, rows = token_refs[0].shape[1:]
    groups = len(token_refs) * token_refs[0].shape[0]
    width, depth = head.shape[0], head_refs[0].shape[-1]
    real, base = plan.columns()

    copies = []
    for source, first, group in plan.head_parts(head_refs):
        target = head.at[pl.ds(first, source.shape[0]), pl.ds(pl.multiple_of(group * depth, LANES), depth)]
        copies.append(pltpu.make_async_copy(source, target, sems.at[len(copies)]))
    for copy in copies:
        copy.start()

    def one_group(group, live):
        def one_sequence(index, load):
            return load + jnp.where(owner_ref[index] == plan.group(group), lens_ref[index], 0)

        load = lax.fori_loop(0, lens_ref.shape[0], one_sequence, jnp.int32(0))
        for split in range(splits):
            order[live] = group * splits + split
            live = live + jnp.where(start_ref[0] + split * rows < load, 1, 0)
        return live

    live = lax.fori_loop(0, groups, one_group, jnp.int32(0))

    def fetch(step, slot):
        group, split = order[step] // splits, order[step] % splits
        each = token_refs[0].shape[0]
        for index, source in enumerate(token_refs):

            @pl.when(group // each == index)
            def _():
                pltpu.make_async_copy(source.at[group % each, split], held.at[slot], token_sems.at[slot]).start()

    @pl.when(live > 0)
    def _():
        fetch(0, 0)

    out_ref[...] = jnp.zeros_like(out_ref)
    for index, source in enumerate(id_refs):
        places = source[...] - base
        ids[pl.ds(index * source.shape[0], source.shape[0])] = jnp.where(places < real, places, -1)
    for copy in copies:
        copy.wait()

    def body(step, carry):
        slot = lax.rem(step, 2)
        pltpu.make_async_copy(token_refs[0].at[0, 0], held.at[slot], token_sems.at[slot]).wait()

        @pl.when(step + 1 < live)
        def _():
            fetch(step + 1, 1 - slot)

        logits[...] = jnp.dot(head[...], held[slot], preferred_element_type=jnp.float32)

        @pl.when(real < width)
        def _():
            column = lax.broadcasted_iota(jnp.int32, (width - plan.least, rows), 0) + plan.least
            logits[plan.least :] = jnp.where(column < real, logits[plan.least :], LOW)

        block = order[step]
        target = plan.slot(block // splits)
        split = block % splits
        column = lax.broadcasted_iota(jnp.int32, (width, LANES), 0)
        for start in range(0, rows, LANES):
            lanes = slice(start, start + LANES)
            values = logits[:, lanes]
            top = jnp.max(values, axis=0, keepdims=True)
            shifted = jnp.maximum(values - top, -1.0e4)
            expo = jnp.exp(shifted)
            total = jnp.sum(expo, axis=0, keepdims=True)
            weighted = jnp.sum(expo * shifted, axis=0, keepdims=True)
            picked = jnp.sum(jnp.where(column == ids[block, :, lanes], values, 0.0), axis=0, keepdims=True)
            place = pl.ds(pl.multiple_of(split * rows + start, LANES), LANES)
            if before:
                top, total, weighted, picked = joined(
                    [(top, total, weighted, picked), [before[0][target, index : index + 1, place] for index in range(4)]]
                )
            for index, member in enumerate((top, total, weighted, picked)):
                out_ref[target, index : index + 1, place] = member
        return carry

    lax.fori_loop(0, live, body, 0)


def stats(plan, start, seq_lens, seq_owner, tokens, ids, heads, before):
    groups, splits, wide, rows = tokens[0].shape
    groups *= len(tokens)
    width = plan.width
    smem = pl.BlockSpec(memory_space=pltpu.SMEM)
    vmem = pl.BlockSpec(memory_space=pltpu.VMEM)
    anywhere = pl.BlockSpec(memory_space=pltpu.HBM)
    return pl.pallas_call(
        functools.partial(stats_kernel, plan, (len(tokens), len(ids), len(heads), len(before))),
        in_specs=[smem] * 3
        + [anywhere] * len(tokens)
        + [vmem] * len(ids)
        + [anywhere] * len(heads)
        + [vmem] * len(before),
        out_specs=vmem,
        scratch_shapes=[
            pltpu.VMEM((width, wide), jnp.bfloat16),
            pltpu.VMEM((2, wide, rows), jnp.bfloat16),
            pltpu.VMEM((width, rows), jnp.float32),
            pltpu.VMEM((groups * splits, 1, rows), jnp.int32),
            pltpu.SMEM((groups * splits + 1,), jnp.int32),
            pltpu.SemaphoreType.DMA((plan.copies,)),
            pltpu.SemaphoreType.DMA((2,)),
        ],
        out_shape=jax.ShapeDtypeStruct((groups, 4, splits * rows), jnp.float32),
        compiler_params=pltpu.CompilerParams(vmem_limit_bytes=60 * 2**20),
        cost_estimate=pl.CostEstimate(
            flops=groups * splits * rows * wide * width // 8,
            bytes_accessed=wide * width,
            transcendentals=groups * splits * rows * width // 8,
        ),
    )(start, seq_lens, seq_owner, *tokens, *ids, *heads, *before)


class Spread:
    def __init__(self, breadth, groups):
        self.breadth = breadth
        self.cuts = [breadth * index // groups // TILE * TILE for index in range(groups)] + [breadth]
        sizes = [end - start for start, end in zip(self.cuts, self.cuts[1:])]
        self.width, self.least = max(sizes), min(sizes)
        self.copies = 1

    def spread(self, turned):
        turned = jnp.pad(turned, ((0, self.cuts[-2] + self.width - self.breadth), (0, 0)))
        return jnp.stack([turned[start : start + self.width] for start in self.cuts[:-1]])

    def columns(self):
        position = lax.axis_index("dp")
        start, end = 0, self.breadth
        for index, (first, last) in enumerate(zip(self.cuts, self.cuts[1:])):
            start = jnp.where(position == index, first, start)
            end = jnp.where(position == index, last, end)
        return end - start, lax.axis_index("vocab") * self.breadth + start

    def head_parts(self, refs):
        return [(refs[0], 0, 0)]

    def group(self, group):
        return group

    def slot(self, group):
        return group


class Line:
    def __init__(self, breadth, chunk, cuts):
        self.breadth, self.chunk, self.cuts = breadth, chunk, cuts
        self.start = cuts[0][0]
        self.width = self.least = sum(width for _, width in cuts)
        self.copies = 2 + 6 * len(cuts)

    def columns(self):
        hi = lax.axis_index("dp") // 2
        return self.width, lax.axis_index("vocab") * self.breadth + hi * self.chunk + self.start

    def head_parts(self, refs):
        position = lax.axis_index("dp")
        hi, low = position // 2, position % 2
        here = pl.ds(self.start, self.width)
        found = [(refs[0].at[hi, here], 0, 2 * hi + low), (refs[1].at[here], 0, 2 * hi + (low ^ 1))]
        for index, (start, _) in enumerate(self.cuts):
            *mine, other = refs[2 + 4 * index : 6 + 4 * index]
            for step in (1, 2, 3):
                found.append((mine[step - 1], start - self.start, 2 * (hi ^ step) + low))
                found.append((other.at[step - 1], start - self.start, 2 * (hi ^ step) + (low ^ 1)))
        return found

    def slot(self, group):
        hi = lax.axis_index("dp") // 2
        middle = (hi == 1) | (hi == 2)
        return jnp.where(middle & (group >= 2), 5 - group, group)

    def group(self, group):
        position = lax.axis_index("dp")
        return 2 * (position // 2 ^ self.slot(group)) + position % 2


def after(x, *others):
    return lax.optimization_barrier((x, *others))[0]


def joined(members):
    best = functools.reduce(jnp.maximum, [top for top, _, _, _ in members])
    total = weighted = picked = 0.0
    for top, other_total, other_weighted, other_picked in members:
        shift = jnp.maximum(top - best, -1.0e4)
        factor = jnp.exp(shift)
        total += other_total * factor
        weighted += factor * (other_weighted + other_total * shift)
        picked += other_picked
    return best, total, weighted, picked


def merge(members):
    return jnp.stack(joined([[member[..., index, :] for index in range(4)] for member in members]), axis=-2)


def by_collectives(hidden, gain, head, target_ids, seq_lens, seq_owner):
    groups = lax.axis_size("dp")
    parts = lax.axis_size("vocab")
    slots, features = hidden.shape
    depth, breadth = head.shape
    plan = Spread(breadth, groups)
    ids = lax.all_gather(target_ids, "dp", axis=0)

    columns = lax.all_to_all(plan.spread(head.T), "dp", split_axis=0, concat_axis=0, tiled=True)
    columns = columns.transpose(1, 0, 2).reshape(plan.width, groups * depth)

    splits = -(-groups * slots * features * parts * 2 // TOKEN_BYTES)
    while slots % splits or (slots // splits) % LANES:
        splits += 1
    rows = slots // splits

    def score(start):
        piece = lax.dynamic_slice_in_dim(hidden, start, rows)
        x = lax.all_gather(piece, ("vocab", "dp"), axis=0).reshape(parts, groups, rows, features)
        x = assemble(gain, [x], rows)
        wanted = lax.dynamic_slice_in_dim(ids, start, rows, axis=1)[:, None]
        return stats(plan, start[None], seq_lens, seq_owner, [x], [wanted], [columns], [])

    found = lax.map(score, jnp.arange(splits, dtype=jnp.int32) * rows)
    found = found.transpose(1, 2, 0, 3).reshape(groups, 4, slots)
    found = lax.all_to_all(found, "dp", split_axis=0, concat_axis=0, tiled=True)
    mine = lax.all_gather(merge(list(found)), "vocab", axis=0)
    return merge(list(mine))


def by_axes(hidden, gain, head, target_ids, seq_lens, seq_owner):
    groups = lax.axis_size("dp")
    parts = lax.axis_size("vocab")
    tall = groups // 2
    hi = lax.axis_index("dp") // 2
    slots, features = hidden.shape
    depth, breadth = head.shape
    splits = slots // ROWS
    middle = (hi == 1) | (hi == 2)
    chunk = breadth // tall
    ends = [chunk * sum(PIECES[:n]) // sum(PIECES) // TILE * TILE for n in range(len(PIECES))] + [chunk]
    cuts = [(start, end - start) for start, end in zip(ends, ends[1:])]

    def swap_hi(x, step):
        return lax.ppermute(x, "dp", [(g, g ^ (2 * step)) for g in range(groups)])

    def swap_lo(x):
        return lax.ppermute(x, "dp", [(g, g ^ 1) for g in range(groups)])

    def swap_part(x, step):
        return lax.ppermute(x, "vocab", [(v, v ^ step) for v in range(parts)])

    def along(x, moves):
        return lax.ppermute(x, "dp", [(2 * a + side, 2 * b + side) for a, b in moves for side in range(2)])

    code = jnp.stack([target_ids >> 8, target_ids & 255]).astype(hidden.dtype).reshape(2, splits, ROWS)
    code = code.transpose(1, 0, 2).reshape(splits, 2 * ROWS)
    own = jnp.concatenate([hidden, jnp.pad(code, ((0, TILE - splits), (0, features - 2 * ROWS)))])
    near = swap_hi(own, 1)
    cross = along(own, [(1, 2), (2, 1)])
    cross_near = along(near, [(1, 2), (2, 1)])
    out = along(cross, [(1, 0), (2, 3)])
    out_near = along(cross_near, [(1, 0), (2, 3)])

    turned = head.T.reshape(tall, chunk, depth)

    def block(step, start, width):
        return lax.dynamic_slice(turned, (hi ^ step, start, 0), (1, width, depth))[0]

    blocks = [[block(step, *cut) for step in (1, 2, 3)] for cut in cuts]

    def to_hi(piece, *others):
        return [swap_hi(after(y, *others), step) for step, y in enumerate(blocks[piece], 1)]

    def over_x(x):
        return swap_part(x, 2)

    def both(x, y, x_across, y_across):
        return jnp.stack([jnp.stack([x, y]), jnp.stack([x_across, y_across])])

    def ready(half, whole):
        code = half[0, :, slots : slots + splits, : 2 * ROWS].astype(jnp.int32).reshape(2 * splits, 2, ROWS)
        return assemble(gain, [half, whole], ROWS), code[:, :1] * 256 + code[:, 1:]

    def score(pieces, before):
        plan = Line(breadth, chunk, [cuts[piece] for piece in pieces])
        heads = [turned, local_block, *(y for piece in pieces for y in (*sent[piece], across[piece]))]
        return stats(plan, jnp.zeros(1, jnp.int32), seq_lens, seq_owner, tokens, ids, heads, before)

    local_block = swap_lo(block(0, 0, chunk))
    own_across = over_x(own)
    near_across = over_x(after(near, cross, own_across, local_block))
    sent = [to_hi(0, out, cross_near, near_across, *blocks[1], *blocks[2])]
    far = jnp.where(middle, cross, out)
    far_across = over_x(far)
    last = jnp.where(middle, cross_near, out_near)
    last_across = over_x(after(last, *sent[0]))
    sent.append(to_hi(1, *sent[0], far_across))
    front_half = both(own, near, own_across, near_across)
    across = [swap_lo(jnp.stack(sent[0]))]
    front = ready(front_half, swap_part(after(front_half, *sent[1], across[0]), 1))
    back_half = both(far, last, far_across, last_across)
    back = ready(back_half, swap_part(after(back_half, *sent[1], across[0]), 1))
    tokens, ids = zip(front, back)
    waits = (tokens[1], sent[1][1], tokens[0])
    sent.append([swap_hi(after(y, *sent[1], wait), step) for step, (y, wait) in enumerate(zip(blocks[2], waits), 1)])
    across.append(swap_lo(jnp.stack(sent[1])))
    across.append(swap_lo(after(jnp.stack(sent[2]), across[1])))
    found = score((2,), [score((0, 1), [])])
    mine = merge([found[0]] + [swap_hi(found[step], step) for step in range(1, tall)])
    return merge([mine] + [swap_part(mine, step) for step in range(1, parts)])


def local(hidden, gain, head, target_ids, seq_lens, seq_owner):
    groups = lax.axis_size("dp")
    slots, features = hidden.shape
    owners = jnp.arange(groups, dtype=jnp.int32)
    loads = jnp.sum(jnp.where(seq_owner[:, None] == owners[None, :], seq_lens[:, None], 0), axis=0).astype(jnp.int32)
    fits = (
        (groups, lax.axis_size("vocab")) == (8, 4)
        and slots % ROWS == 0
        and slots // ROWS <= TILE
        and 2 * ROWS <= features
        and head.shape[1] % (groups // 2 * TILE) == 0
    )
    transport = by_axes if fits else by_collectives
    scores = transport(hidden, gain.astype(jnp.float32)[None], head, target_ids, seq_lens, seq_owner)
    top, total, weighted, picked = (scores[index] for index in range(4))
    spread = jnp.log(total)
    logprob = picked - (top + spread)
    entropy = spread - weighted / total
    live = jnp.arange(slots, dtype=jnp.int32) < loads[lax.axis_index("dp")]
    return (jnp.where(live, logprob, 0.0), jnp.where(live, entropy, 0.0))


def solution(mesh):
    return jax.shard_map(
        local,
        mesh=mesh,
        in_specs=(P("dp", "vocab"), P(), P("dp", "vocab"), P("dp"), P(), P()),
        out_specs=(P("dp"), P("dp")),
        check_vma=False,
    )
```

```python
import functools

import jax
import jax.numpy as jnp
from jax import lax
from jax.experimental import pallas as pl
from jax.experimental.pallas import tpu as pltpu
from jax.sharding import PartitionSpec as P

EPS = 1e-05
LOW = -3.0e38
LANES = 128
TILE = 16
PIECES = (8, 7, 5)
ROWS = 256
TOKEN_BYTES = 17 * 2**20


def assemble_kernel(near_first, gain_ref, *refs):
    target = refs[-1]
    sources = []
    for away, ref in enumerate(refs[:-1]):
        for index in range(ref.shape[0]):
            part = lax.axis_index("vocab") ^ (2 * index + away) if near_first else index
            sources.append((ref, index, part))
    features = refs[0].shape[3]
    for start in range(0, target.shape[3], LANES):
        lanes = slice(start, start + LANES)
        square = sum(
            jnp.sum(jnp.square(ref[at, 0, lanes].astype(jnp.float32)), axis=1, keepdims=True) for ref, at, _ in sources
        )
        scale = lax.rsqrt(square / (features * len(sources)) + EPS)
        for ref, at, part in sources:
            first = pl.multiple_of(part * features, features)
            value = ref[at, 0, lanes].astype(jnp.float32) * scale * gain_ref[:, pl.ds(first, features)]
            target[0, 0, pl.ds(first, features), lanes] = value.T.astype(target.dtype)


def assemble(gain, sources, rows):
    _, count, slots, features = sources[0].shape
    splits = slots // rows
    wide = features * sum(y.shape[0] for y in sources)
    return pl.pallas_call(
        functools.partial(assemble_kernel, len(sources) > 1),
        grid=(count, splits),
        in_specs=[pl.BlockSpec((1, wide), lambda i, j: (0, 0))]
        + [pl.BlockSpec((y.shape[0], 1, rows, features), lambda i, j: (0, i, j, 0)) for y in sources],
        out_specs=pl.BlockSpec((1, 1, wide, rows), lambda i, j: (i, j, 0, 0)),
        out_shape=jax.ShapeDtypeStruct((count, splits, wide, rows), sources[0].dtype),
        compiler_params=pltpu.CompilerParams(vmem_limit_bytes=60 * 2**20),
        cost_estimate=pl.CostEstimate(
            flops=6 * count * splits * rows * wide,
            bytes_accessed=4 * count * splits * rows * wide,
            transcendentals=count * splits * rows,
        ),
    )(gain, *sources)


def stats_kernel(plan, counts, start_ref, lens_ref, owner_ref, *refs):
    out_ref, head, held, logits, ids, order, sems, token_sems = refs[-8:]
    members = []
    for count in counts:
        members.append(refs[:count])
        refs = refs[count:]
    token_refs, id_refs, head_refs, before = members
    splits, _, rows = token_refs[0].shape[1:]
    groups = len(token_refs) * token_refs[0].shape[0]
    width, depth = head.shape[0], head_refs[0].shape[-1]
    real, base = plan.columns()

    copies = []
    for source, first, group in plan.head_parts(head_refs):
        target = head.at[pl.ds(first, source.shape[0]), pl.ds(pl.multiple_of(group * depth, LANES), depth)]
        copies.append(pltpu.make_async_copy(source, target, sems.at[len(copies)]))
    for copy in copies:
        copy.start()

    def one_group(group, live):
        def one_sequence(index, load):
            return load + jnp.where(owner_ref[index] == plan.group(group), lens_ref[index], 0)

        load = lax.fori_loop(0, lens_ref.shape[0], one_sequence, jnp.int32(0))
        for split in range(splits):
            order[live] = group * splits + split
            live = live + jnp.where(start_ref[0] + split * rows < load, 1, 0)
        return live

    live = lax.fori_loop(0, groups, one_group, jnp.int32(0))

    def fetch(step, slot):
        group, split = order[step] // splits, order[step] % splits
        each = token_refs[0].shape[0]
        for index, source in enumerate(token_refs):

            @pl.when(group // each == index)
            def _():
                for first in range(0, held.shape[1], held.shape[1] // 4):
                    part = pl.ds(first, held.shape[1] // 4)
                    pltpu.make_async_copy(
                        source.at[group % each, split, part], held.at[slot, part], token_sems.at[slot]
                    ).start()

    @pl.when(live > 0)
    def _():
        fetch(0, 0)

    out_ref[...] = jnp.zeros_like(out_ref)
    for index, source in enumerate(id_refs):
        places = source[...] - base
        ids[pl.ds(index * source.shape[0], source.shape[0])] = jnp.where(places < real, places, -1)
    for copy in copies:
        copy.wait()

    def body(step, carry):
        slot = lax.rem(step, 2)
        pltpu.make_async_copy(token_refs[0].at[0, 0], held.at[slot], token_sems.at[slot]).wait()

        @pl.when(step + 1 < live)
        def _():
            fetch(step + 1, 1 - slot)

        logits[...] = jnp.dot(head[...], held[slot], preferred_element_type=jnp.float32)

        @pl.when(real < width)
        def _():
            column = lax.broadcasted_iota(jnp.int32, (width - plan.least, rows), 0) + plan.least
            logits[plan.least :] = jnp.where(column < real, logits[plan.least :], LOW)

        block = order[step]
        target = plan.slot(block // splits)
        split = block % splits
        column = lax.broadcasted_iota(jnp.int32, (width, LANES), 0)
        for start in range(0, rows, LANES):
            lanes = slice(start, start + LANES)
            values = logits[:, lanes]
            top = jnp.max(values, axis=0, keepdims=True)
            shifted = jnp.maximum(values - top, -1.0e4)
            expo = jnp.exp(shifted)
            total = jnp.sum(expo, axis=0, keepdims=True)
            weighted = jnp.sum(expo * shifted, axis=0, keepdims=True)
            picked = jnp.sum(jnp.where(column == ids[block, :, lanes], values, 0.0), axis=0, keepdims=True)
            place = pl.ds(pl.multiple_of(split * rows + start, LANES), LANES)
            if before:
                top, total, weighted, picked = joined(
                    [(top, total, weighted, picked), [before[0][target, index : index + 1, place] for index in range(4)]]
                )
            for index, member in enumerate((top, total, weighted, picked)):
                out_ref[target, index : index + 1, place] = member
        return carry

    lax.fori_loop(0, live, body, 0)


def stats(plan, start, seq_lens, seq_owner, tokens, ids, heads, before):
    groups, splits, wide, rows = tokens[0].shape
    groups *= len(tokens)
    width = plan.width
    smem = pl.BlockSpec(memory_space=pltpu.SMEM)
    vmem = pl.BlockSpec(memory_space=pltpu.VMEM)
    anywhere = pl.BlockSpec(memory_space=pltpu.HBM)
    return pl.pallas_call(
        functools.partial(stats_kernel, plan, (len(tokens), len(ids), len(heads), len(before))),
        in_specs=[smem] * 3
        + [anywhere] * len(tokens)
        + [vmem] * len(ids)
        + [anywhere] * len(heads)
        + [vmem] * len(before),
        out_specs=vmem,
        scratch_shapes=[
            pltpu.VMEM((width, wide), jnp.bfloat16),
            pltpu.VMEM((2, wide, rows), jnp.bfloat16),
            pltpu.VMEM((width, rows), jnp.float32),
            pltpu.VMEM((groups * splits, 1, rows), jnp.int32),
            pltpu.SMEM((groups * splits + 1,), jnp.int32),
            pltpu.SemaphoreType.DMA((plan.copies,)),
            pltpu.SemaphoreType.DMA((2,)),
        ],
        out_shape=jax.ShapeDtypeStruct((groups, 4, splits * rows), jnp.float32),
        compiler_params=pltpu.CompilerParams(vmem_limit_bytes=60 * 2**20),
        cost_estimate=pl.CostEstimate(
            flops=groups * splits * rows * wide * width // 8,
            bytes_accessed=wide * width,
            transcendentals=groups * splits * rows * width // 8,
        ),
    )(start, seq_lens, seq_owner, *tokens, *ids, *heads, *before)


class Spread:
    def __init__(self, breadth, groups):
        self.breadth = breadth
        self.cuts = [breadth * index // groups // TILE * TILE for index in range(groups)] + [breadth]
        sizes = [end - start for start, end in zip(self.cuts, self.cuts[1:])]
        self.width, self.least = max(sizes), min(sizes)
        self.copies = 1

    def spread(self, turned):
        turned = jnp.pad(turned, ((0, self.cuts[-2] + self.width - self.breadth), (0, 0)))
        return jnp.stack([turned[start : start + self.width] for start in self.cuts[:-1]])

    def columns(self):
        position = lax.axis_index("dp")
        start, end = 0, self.breadth
        for index, (first, last) in enumerate(zip(self.cuts, self.cuts[1:])):
            start = jnp.where(position == index, first, start)
            end = jnp.where(position == index, last, end)
        return end - start, lax.axis_index("vocab") * self.breadth + start

    def head_parts(self, refs):
        return [(refs[0], 0, 0)]

    def group(self, group):
        return group

    def slot(self, group):
        return group


class Line:
    def __init__(self, breadth, chunk, cuts):
        self.breadth, self.chunk, self.cuts = breadth, chunk, cuts
        self.start = cuts[0][0]
        self.width = self.least = sum(width for _, width in cuts)
        self.copies = 2 + 6 * len(cuts)

    def columns(self):
        hi = lax.axis_index("dp") // 2
        return self.width, lax.axis_index("vocab") * self.breadth + hi * self.chunk + self.start

    def head_parts(self, refs):
        position = lax.axis_index("dp")
        hi, low = position // 2, position % 2
        here = pl.ds(self.start, self.width)
        found = [(refs[0].at[hi, here], 0, 2 * hi + low), (refs[1].at[here], 0, 2 * hi + (low ^ 1))]
        for index, (start, _) in enumerate(self.cuts):
            *mine, other = refs[2 + 4 * index : 6 + 4 * index]
            for step in (1, 2, 3):
                found.append((mine[step - 1], start - self.start, 2 * (hi ^ step) + low))
                found.append((other.at[step - 1], start - self.start, 2 * (hi ^ step) + (low ^ 1)))
        return found

    def slot(self, group):
        hi = lax.axis_index("dp") // 2
        middle = (hi == 1) | (hi == 2)
        return jnp.where(middle & (group >= 2), 5 - group, group)

    def group(self, group):
        position = lax.axis_index("dp")
        return 2 * (position // 2 ^ self.slot(group)) + position % 2


def after(x, *others):
    return lax.optimization_barrier((x, *others))[0]


def joined(members):
    best = functools.reduce(jnp.maximum, [top for top, _, _, _ in members])
    total = weighted = picked = 0.0
    for top, other_total, other_weighted, other_picked in members:
        shift = jnp.maximum(top - best, -1.0e4)
        factor = jnp.exp(shift)
        total += other_total * factor
        weighted += factor * (other_weighted + other_total * shift)
        picked += other_picked
    return best, total, weighted, picked


def merge(members):
    return jnp.stack(joined([[member[..., index, :] for index in range(4)] for member in members]), axis=-2)


def by_collectives(hidden, gain, head, target_ids, seq_lens, seq_owner):
    groups = lax.axis_size("dp")
    parts = lax.axis_size("vocab")
    slots, features = hidden.shape
    depth, breadth = head.shape
    plan = Spread(breadth, groups)
    ids = lax.all_gather(target_ids, "dp", axis=0)

    columns = lax.all_to_all(plan.spread(head.T), "dp", split_axis=0, concat_axis=0, tiled=True)
    columns = columns.transpose(1, 0, 2).reshape(plan.width, groups * depth)

    splits = -(-groups * slots * features * parts * 2 // TOKEN_BYTES)
    while slots % splits or (slots // splits) % LANES:
        splits += 1
    rows = slots // splits

    def score(start):
        piece = lax.dynamic_slice_in_dim(hidden, start, rows)
        x = lax.all_gather(piece, ("vocab", "dp"), axis=0).reshape(parts, groups, rows, features)
        x = assemble(gain, [x], rows)
        wanted = lax.dynamic_slice_in_dim(ids, start, rows, axis=1)[:, None]
        return stats(plan, start[None], seq_lens, seq_owner, [x], [wanted], [columns], [])

    found = lax.map(score, jnp.arange(splits, dtype=jnp.int32) * rows)
    found = found.transpose(1, 2, 0, 3).reshape(groups, 4, slots)
    found = lax.all_to_all(found, "dp", split_axis=0, concat_axis=0, tiled=True)
    mine = lax.all_gather(merge(list(found)), "vocab", axis=0)
    return merge(list(mine))


def by_axes(hidden, gain, head, target_ids, seq_lens, seq_owner):
    groups = lax.axis_size("dp")
    parts = lax.axis_size("vocab")
    tall = groups // 2
    hi = lax.axis_index("dp") // 2
    slots, features = hidden.shape
    depth, breadth = head.shape
    splits = slots // ROWS
    middle = (hi == 1) | (hi == 2)
    chunk = breadth // tall
    ends = [chunk * sum(PIECES[:n]) // sum(PIECES) // TILE * TILE for n in range(len(PIECES))] + [chunk]
    cuts = [(start, end - start) for start, end in zip(ends, ends[1:])]

    def swap_hi(x, step):
        return lax.ppermute(x, "dp", [(g, g ^ (2 * step)) for g in range(groups)])

    def swap_lo(x):
        return lax.ppermute(x, "dp", [(g, g ^ 1) for g in range(groups)])

    def swap_part(x, step):
        return lax.ppermute(x, "vocab", [(v, v ^ step) for v in range(parts)])

    def along(x, moves):
        return lax.ppermute(x, "dp", [(2 * a + side, 2 * b + side) for a, b in moves for side in range(2)])

    code = jnp.stack([target_ids >> 8, target_ids & 255]).astype(hidden.dtype).reshape(2, splits, ROWS)
    code = code.transpose(1, 0, 2).reshape(splits, 2 * ROWS)
    own = jnp.concatenate([hidden, jnp.pad(code, ((0, TILE - splits), (0, features - 2 * ROWS)))])
    near = swap_hi(own, 1)
    cross = along(own, [(1, 2), (2, 1)])
    cross_near = along(near, [(1, 2), (2, 1)])
    out = along(cross, [(1, 0), (2, 3)])
    out_near = along(cross_near, [(1, 0), (2, 3)])

    turned = head.T.reshape(tall, chunk, depth)

    def block(step, start, width):
        return lax.dynamic_slice(turned, (hi ^ step, start, 0), (1, width, depth))[0]

    blocks = [[block(step, *cut) for step in (1, 2, 3)] for cut in cuts]

    def to_hi(piece, *others):
        return [swap_hi(after(y, *others), step) for step, y in enumerate(blocks[piece], 1)]

    def over_x(x):
        return swap_part(x, 2)

    def both(x, y, x_across, y_across):
        return jnp.stack([jnp.stack([x, y]), jnp.stack([x_across, y_across])])

    def ready(half, whole):
        code = half[0, :, slots : slots + splits, : 2 * ROWS].astype(jnp.int32).reshape(2 * splits, 2, ROWS)
        return assemble(gain, [half, whole], ROWS), code[:, :1] * 256 + code[:, 1:]

    def score(pieces, before):
        plan = Line(breadth, chunk, [cuts[piece] for piece in pieces])
        heads = [turned, local_block, *(y for piece in pieces for y in (*sent[piece], across[piece]))]
        return stats(plan, jnp.zeros(1, jnp.int32), seq_lens, seq_owner, tokens, ids, heads, before)

    local_block = swap_lo(block(0, 0, chunk))
    own_across = over_x(own)
    near_across = over_x(after(near, cross, own_across, local_block))
    sent = [to_hi(0, out, cross_near, near_across, *blocks[1], *blocks[2])]
    far = jnp.where(middle, cross, out)
    far_across = over_x(far)
    last = jnp.where(middle, cross_near, out_near)
    last_across = over_x(after(last, *sent[0]))
    sent.append(to_hi(1, *sent[0], far_across))
    front_half = both(own, near, own_across, near_across)
    across = [swap_lo(jnp.stack(sent[0]))]
    front = ready(front_half, swap_part(after(front_half, *sent[1], across[0]), 1))
    back_half = both(far, last, far_across, last_across)
    back = ready(back_half, swap_part(after(back_half, *sent[1], across[0]), 1))
    tokens, ids = zip(front, back)
    waits = (tokens[0], sent[1][1], sent[1][2])
    sent.append([swap_hi(after(y, *sent[1], wait), step) for step, (y, wait) in enumerate(zip(blocks[2], waits), 1)])
    across.append(swap_lo(jnp.stack(sent[1])))
    across.append(swap_lo(after(jnp.stack(sent[2]), across[1])))
    found = score((2,), [score((0, 1), [])])
    mine = merge([found[0]] + [swap_hi(found[step], step) for step in range(1, tall)])
    return merge([mine] + [swap_part(mine, step) for step in range(1, parts)])


def local(hidden, gain, head, target_ids, seq_lens, seq_owner):
    groups = lax.axis_size("dp")
    slots, features = hidden.shape
    owners = jnp.arange(groups, dtype=jnp.int32)
    loads = jnp.sum(jnp.where(seq_owner[:, None] == owners[None, :], seq_lens[:, None], 0), axis=0).astype(jnp.int32)
    fits = (
        (groups, lax.axis_size("vocab")) == (8, 4)
        and slots % ROWS == 0
        and slots // ROWS <= TILE
        and 2 * ROWS <= features
        and head.shape[1] % (groups // 2 * TILE) == 0
    )
    transport = by_axes if fits else by_collectives
    scores = transport(hidden, gain.astype(jnp.float32)[None], head, target_ids, seq_lens, seq_owner)
    top, total, weighted, picked = (scores[index] for index in range(4))
    spread = jnp.log(total)
    logprob = picked - (top + spread)
    entropy = spread - weighted / total
    live = jnp.arange(slots, dtype=jnp.int32) < loads[lax.axis_index("dp")]
    return (jnp.where(live, logprob, 0.0), jnp.where(live, entropy, 0.0))


def solution(mesh):
    return jax.shard_map(
        local,
        mesh=mesh,
        in_specs=(P("dp", "vocab"), P(), P("dp", "vocab"), P("dp"), P(), P()),
        out_specs=(P("dp"), P("dp")),
        check_vma=False,
    )
```

```python
import functools

import jax
import jax.numpy as jnp
from jax import lax
from jax.experimental import pallas as pl
from jax.experimental.pallas import tpu as pltpu
from jax.sharding import PartitionSpec as P

EPS = 1e-05
LOW = -3.0e38
LANES = 128
TILE = 16
PIECES = (8, 7, 5)
ROWS = 256
TOKEN_BYTES = 17 * 2**20


def assemble_kernel(near_first, gain_ref, *refs):
    target = refs[-1]
    sources = []
    for away, ref in enumerate(refs[:-1]):
        for index in range(ref.shape[0]):
            part = lax.axis_index("vocab") ^ (2 * index + away) if near_first else index
            sources.append((ref, index, part))
    features = refs[0].shape[3]
    for start in range(0, target.shape[3], LANES):
        lanes = slice(start, start + LANES)
        square = sum(
            jnp.sum(jnp.square(ref[at, 0, lanes].astype(jnp.float32)), axis=1, keepdims=True) for ref, at, _ in sources
        )
        scale = lax.rsqrt(square / (features * len(sources)) + EPS)
        for ref, at, part in sources:
            first = pl.multiple_of(part * features, features)
            value = ref[at, 0, lanes].astype(jnp.float32) * scale * gain_ref[:, pl.ds(first, features)]
            target[0, 0, pl.ds(first, features), lanes] = value.T.astype(target.dtype)


def assemble(gain, sources, rows):
    _, count, slots, features = sources[0].shape
    splits = slots // rows
    wide = features * sum(y.shape[0] for y in sources)
    return pl.pallas_call(
        functools.partial(assemble_kernel, len(sources) > 1),
        grid=(count, splits),
        in_specs=[pl.BlockSpec((1, wide), lambda i, j: (0, 0))]
        + [pl.BlockSpec((y.shape[0], 1, rows, features), lambda i, j: (0, i, j, 0)) for y in sources],
        out_specs=pl.BlockSpec((1, 1, wide, rows), lambda i, j: (i, j, 0, 0)),
        out_shape=jax.ShapeDtypeStruct((count, splits, wide, rows), sources[0].dtype),
        compiler_params=pltpu.CompilerParams(vmem_limit_bytes=60 * 2**20),
        cost_estimate=pl.CostEstimate(
            flops=6 * count * splits * rows * wide,
            bytes_accessed=4 * count * splits * rows * wide,
            transcendentals=count * splits * rows,
        ),
    )(gain, *sources)


def stats_kernel(plan, counts, start_ref, lens_ref, owner_ref, *refs):
    out_ref, head, held, logits, ids, order, sems, token_sems = refs[-8:]
    members = []
    for count in counts:
        members.append(refs[:count])
        refs = refs[count:]
    token_refs, id_refs, head_refs, before = members
    splits, _, rows = token_refs[0].shape[1:]
    groups = len(token_refs) * token_refs[0].shape[0]
    width, depth = head.shape[0], head_refs[0].shape[-1]
    real, base = plan.columns()

    copies = []
    for source, first, group in plan.head_parts(head_refs):
        target = head.at[pl.ds(first, source.shape[0]), pl.ds(pl.multiple_of(group * depth, LANES), depth)]
        copies.append(pltpu.make_async_copy(source, target, sems.at[len(copies)]))
    for copy in copies:
        copy.start()

    def one_group(group, live):
        def one_sequence(index, load):
            return load + jnp.where(owner_ref[index] == plan.group(group), lens_ref[index], 0)

        load = lax.fori_loop(0, lens_ref.shape[0], one_sequence, jnp.int32(0))
        for split in range(splits):
            order[live] = group * splits + split
            live = live + jnp.where(start_ref[0] + split * rows < load, 1, 0)
        return live

    live = lax.fori_loop(0, groups, one_group, jnp.int32(0))

    def fetch(step, slot):
        group, split = order[step] // splits, order[step] % splits
        each = token_refs[0].shape[0]
        for index, source in enumerate(token_refs):

            @pl.when(group // each == index)
            def _():
                for first in range(0, held.shape[1], held.shape[1] // 4):
                    part = pl.ds(first, held.shape[1] // 4)
                    pltpu.make_async_copy(
                        source.at[group % each, split, part], held.at[slot, part], token_sems.at[slot]
                    ).start()

    @pl.when(live > 0)
    def _():
        fetch(0, 0)

    out_ref[...] = jnp.zeros_like(out_ref)
    for index, source in enumerate(id_refs):
        places = source[...] - base
        ids[pl.ds(index * source.shape[0], source.shape[0])] = jnp.where(places < real, places, -1)
    for copy in copies:
        copy.wait()

    def body(step, carry):
        slot = lax.rem(step, 2)
        pltpu.make_async_copy(token_refs[0].at[0, 0], held.at[slot], token_sems.at[slot]).wait()

        @pl.when(step + 1 < live)
        def _():
            fetch(step + 1, 1 - slot)

        logits[...] = jnp.dot(head[...], held[slot], preferred_element_type=jnp.float32)

        @pl.when(real < width)
        def _():
            column = lax.broadcasted_iota(jnp.int32, (width - plan.least, rows), 0) + plan.least
            logits[plan.least :] = jnp.where(column < real, logits[plan.least :], LOW)

        block = order[step]
        target = plan.slot(block // splits)
        split = block % splits
        column = lax.broadcasted_iota(jnp.int32, (width, LANES), 0)
        for start in range(0, rows, LANES):
            lanes = slice(start, start + LANES)
            values = logits[:, lanes]
            top = jnp.max(values, axis=0, keepdims=True)
            shifted = jnp.maximum(values - top, -1.0e4)
            expo = jnp.exp(shifted)
            total = jnp.sum(expo, axis=0, keepdims=True)
            weighted = jnp.sum(expo * shifted, axis=0, keepdims=True)
            picked = jnp.sum(jnp.where(column == ids[block, :, lanes], values, 0.0), axis=0, keepdims=True)
            place = pl.ds(pl.multiple_of(split * rows + start, LANES), LANES)
            if before:
                top, total, weighted, picked = joined(
                    [(top, total, weighted, picked), [before[0][target, index : index + 1, place] for index in range(4)]]
                )
            for index, member in enumerate((top, total, weighted, picked)):
                out_ref[target, index : index + 1, place] = member
        return carry

    lax.fori_loop(0, live, body, 0)


def stats(plan, start, seq_lens, seq_owner, tokens, ids, heads, before):
    groups, splits, wide, rows = tokens[0].shape
    groups *= len(tokens)
    width = plan.width
    smem = pl.BlockSpec(memory_space=pltpu.SMEM)
    vmem = pl.BlockSpec(memory_space=pltpu.VMEM)
    anywhere = pl.BlockSpec(memory_space=pltpu.HBM)
    return pl.pallas_call(
        functools.partial(stats_kernel, plan, (len(tokens), len(ids), len(heads), len(before))),
        in_specs=[smem] * 3
        + [anywhere] * len(tokens)
        + [vmem] * len(ids)
        + [anywhere] * len(heads)
        + [vmem] * len(before),
        out_specs=vmem,
        scratch_shapes=[
            pltpu.VMEM((width, wide), jnp.bfloat16),
            pltpu.VMEM((2, wide, rows), jnp.bfloat16),
            pltpu.VMEM((width, rows), jnp.float32),
            pltpu.VMEM((groups * splits, 1, rows), jnp.int32),
            pltpu.SMEM((groups * splits + 1,), jnp.int32),
            pltpu.SemaphoreType.DMA((plan.copies,)),
            pltpu.SemaphoreType.DMA((2,)),
        ],
        out_shape=jax.ShapeDtypeStruct((groups, 4, splits * rows), jnp.float32),
        compiler_params=pltpu.CompilerParams(vmem_limit_bytes=60 * 2**20),
        cost_estimate=pl.CostEstimate(
            flops=groups * splits * rows * wide * width // 8,
            bytes_accessed=wide * width,
            transcendentals=groups * splits * rows * width // 8,
        ),
    )(start, seq_lens, seq_owner, *tokens, *ids, *heads, *before)


class Spread:
    def __init__(self, breadth, groups):
        self.breadth = breadth
        self.cuts = [breadth * index // groups // TILE * TILE for index in range(groups)] + [breadth]
        sizes = [end - start for start, end in zip(self.cuts, self.cuts[1:])]
        self.width, self.least = max(sizes), min(sizes)
        self.copies = 1

    def spread(self, turned):
        turned = jnp.pad(turned, ((0, self.cuts[-2] + self.width - self.breadth), (0, 0)))
        return jnp.stack([turned[start : start + self.width] for start in self.cuts[:-1]])

    def columns(self):
        position = lax.axis_index("dp")
        start, end = 0, self.breadth
        for index, (first, last) in enumerate(zip(self.cuts, self.cuts[1:])):
            start = jnp.where(position == index, first, start)
            end = jnp.where(position == index, last, end)
        return end - start, lax.axis_index("vocab") * self.breadth + start

    def head_parts(self, refs):
        return [(refs[0], 0, 0)]

    def group(self, group):
        return group

    def slot(self, group):
        return group


class Line:
    def __init__(self, breadth, chunk, cuts):
        self.breadth, self.chunk, self.cuts = breadth, chunk, cuts
        self.start = cuts[0][0]
        self.width = self.least = sum(width for _, width in cuts)
        self.copies = 2 + 6 * len(cuts)

    def columns(self):
        hi = lax.axis_index("dp") // 2
        return self.width, lax.axis_index("vocab") * self.breadth + hi * self.chunk + self.start

    def head_parts(self, refs):
        position = lax.axis_index("dp")
        hi, low = position // 2, position % 2
        here = pl.ds(self.start, self.width)
        found = [(refs[0].at[hi, here], 0, 2 * hi + low), (refs[1].at[here], 0, 2 * hi + (low ^ 1))]
        for index, (start, _) in enumerate(self.cuts):
            *mine, other = refs[2 + 4 * index : 6 + 4 * index]
            for step in (1, 2, 3):
                found.append((mine[step - 1], start - self.start, 2 * (hi ^ step) + low))
                found.append((other.at[step - 1], start - self.start, 2 * (hi ^ step) + (low ^ 1)))
        return found

    def slot(self, group):
        hi = lax.axis_index("dp") // 2
        middle = (hi == 1) | (hi == 2)
        return jnp.where(middle & (group >= 2), 5 - group, group)

    def group(self, group):
        position = lax.axis_index("dp")
        return 2 * (position // 2 ^ self.slot(group)) + position % 2


def after(x, *others):
    return lax.optimization_barrier((x, *others))[0]


def joined(members):
    best = functools.reduce(jnp.maximum, [top for top, _, _, _ in members])
    total = weighted = picked = 0.0
    for top, other_total, other_weighted, other_picked in members:
        shift = jnp.maximum(top - best, -1.0e4)
        factor = jnp.exp(shift)
        total += other_total * factor
        weighted += factor * (other_weighted + other_total * shift)
        picked += other_picked
    return best, total, weighted, picked


def merge(members):
    return jnp.stack(joined([[member[..., index, :] for index in range(4)] for member in members]), axis=-2)


def by_collectives(hidden, gain, head, target_ids, seq_lens, seq_owner):
    groups = lax.axis_size("dp")
    parts = lax.axis_size("vocab")
    slots, features = hidden.shape
    depth, breadth = head.shape
    plan = Spread(breadth, groups)
    ids = lax.all_gather(target_ids, "dp", axis=0)

    columns = lax.all_to_all(plan.spread(head.T), "dp", split_axis=0, concat_axis=0, tiled=True)
    columns = columns.transpose(1, 0, 2).reshape(plan.width, groups * depth)

    splits = -(-groups * slots * features * parts * 2 // TOKEN_BYTES)
    while slots % splits or (slots // splits) % LANES:
        splits += 1
    rows = slots // splits

    def score(start):
        piece = lax.dynamic_slice_in_dim(hidden, start, rows)
        x = lax.all_gather(piece, ("vocab", "dp"), axis=0).reshape(parts, groups, rows, features)
        x = assemble(gain, [x], rows)
        wanted = lax.dynamic_slice_in_dim(ids, start, rows, axis=1)[:, None]
        return stats(plan, start[None], seq_lens, seq_owner, [x], [wanted], [columns], [])

    found = lax.map(score, jnp.arange(splits, dtype=jnp.int32) * rows)
    found = found.transpose(1, 2, 0, 3).reshape(groups, 4, slots)
    found = lax.all_to_all(found, "dp", split_axis=0, concat_axis=0, tiled=True)
    mine = lax.all_gather(merge(list(found)), "vocab", axis=0)
    return merge(list(mine))


def by_axes(hidden, gain, head, target_ids, seq_lens, seq_owner):
    groups = lax.axis_size("dp")
    parts = lax.axis_size("vocab")
    tall = groups // 2
    hi = lax.axis_index("dp") // 2
    slots, features = hidden.shape
    depth, breadth = head.shape
    splits = slots // ROWS
    middle = (hi == 1) | (hi == 2)
    chunk = breadth // tall
    ends = [chunk * sum(PIECES[:n]) // sum(PIECES) // TILE * TILE for n in range(len(PIECES))] + [chunk]
    cuts = [(start, end - start) for start, end in zip(ends, ends[1:])]

    def swap_hi(x, step):
        return lax.ppermute(x, "dp", [(g, g ^ (2 * step)) for g in range(groups)])

    def swap_lo(x):
        return lax.ppermute(x, "dp", [(g, g ^ 1) for g in range(groups)])

    def swap_part(x, step):
        return lax.ppermute(x, "vocab", [(v, v ^ step) for v in range(parts)])

    def along(x, moves):
        return lax.ppermute(x, "dp", [(2 * a + side, 2 * b + side) for a, b in moves for side in range(2)])

    code = jnp.stack([target_ids >> 8, target_ids & 255]).astype(hidden.dtype).reshape(2, splits, ROWS)
    code = code.transpose(1, 0, 2).reshape(splits, 2 * ROWS)
    own = jnp.concatenate([hidden, jnp.pad(code, ((0, TILE - splits), (0, features - 2 * ROWS)))])
    near = swap_hi(own, 1)
    cross = along(own, [(1, 2), (2, 1)])
    cross_near = along(near, [(1, 2), (2, 1)])
    out = along(cross, [(1, 0), (2, 3)])
    out_near = along(cross_near, [(1, 0), (2, 3)])

    turned = head.T.reshape(tall, chunk, depth)

    def block(step, start, width):
        return lax.dynamic_slice(turned, (hi ^ step, start, 0), (1, width, depth))[0]

    blocks = [[block(step, *cut) for step in (1, 2, 3)] for cut in cuts]

    def to_hi(piece, *others):
        return [swap_hi(after(y, *others), step) for step, y in enumerate(blocks[piece], 1)]

    def over_x(x):
        return swap_part(x, 2)

    def both(x, y, x_across, y_across):
        return jnp.stack([jnp.stack([x, y]), jnp.stack([x_across, y_across])])

    def ready(half, whole):
        code = half[0, :, slots : slots + splits, : 2 * ROWS].astype(jnp.int32).reshape(2 * splits, 2, ROWS)
        return assemble(gain, [half, whole], ROWS), code[:, :1] * 256 + code[:, 1:]

    def score(pieces, before):
        plan = Line(breadth, chunk, [cuts[piece] for piece in pieces])
        heads = [turned, local_block, *(y for piece in pieces for y in (*sent[piece], across[piece]))]
        return stats(plan, jnp.zeros(1, jnp.int32), seq_lens, seq_owner, tokens, ids, heads, before)

    local_block = swap_lo(block(0, 0, chunk))
    own_across = over_x(own)
    near_across = over_x(after(near, cross, own_across, local_block))
    sent = [to_hi(0, out, cross_near, near_across, *blocks[1], *blocks[2])]
    far = jnp.where(middle, cross, out)
    far_across = over_x(far)
    last = jnp.where(middle, cross_near, out_near)
    last_across = over_x(after(last, *sent[0]))
    sent.append(to_hi(1, *sent[0], far_across))
    front_half = both(own, near, own_across, near_across)
    across = [swap_lo(jnp.stack(sent[0]))]
    front = ready(front_half, swap_part(after(front_half, *sent[1], across[0]), 1))
    back_half = both(far, last, far_across, last_across)
    back = ready(back_half, swap_part(after(back_half, *sent[1], across[0]), 1))
    tokens, ids = zip(front, back)
    waits = (tokens, [], [])
    sent.append([swap_hi(after(y, *sent[1], *wait), step) for step, (y, wait) in enumerate(zip(blocks[2], waits), 1)])
    across.append(swap_lo(jnp.stack(sent[1])))
    across.append(swap_lo(after(jnp.stack(sent[2]), across[1])))
    found = score((2,), [score((0, 1), [])])
    mine = merge([found[0]] + [swap_hi(found[step], step) for step in range(1, tall)])
    return merge([mine] + [swap_part(mine, step) for step in range(1, parts)])


def local(hidden, gain, head, target_ids, seq_lens, seq_owner):
    groups = lax.axis_size("dp")
    slots, features = hidden.shape
    owners = jnp.arange(groups, dtype=jnp.int32)
    loads = jnp.sum(jnp.where(seq_owner[:, None] == owners[None, :], seq_lens[:, None], 0), axis=0).astype(jnp.int32)
    fits = (
        (groups, lax.axis_size("vocab")) == (8, 4)
        and slots % ROWS == 0
        and slots // ROWS <= TILE
        and 2 * ROWS <= features
        and head.shape[1] % (groups // 2 * TILE) == 0
    )
    transport = by_axes if fits else by_collectives
    scores = transport(hidden, gain.astype(jnp.float32)[None], head, target_ids, seq_lens, seq_owner)
    top, total, weighted, picked = (scores[index] for index in range(4))
    spread = jnp.log(total)
    logprob = picked - (top + spread)
    entropy = spread - weighted / total
    live = jnp.arange(slots, dtype=jnp.int32) < loads[lax.axis_index("dp")]
    return (jnp.where(live, logprob, 0.0), jnp.where(live, entropy, 0.0))


def solution(mesh):
    return jax.shard_map(
        local,
        mesh=mesh,
        in_specs=(P("dp", "vocab"), P(), P("dp", "vocab"), P("dp"), P(), P()),
        out_specs=(P("dp"), P("dp")),
        check_vma=False,
    )
```

```python
import functools

import jax
import jax.numpy as jnp
from jax import lax
from jax.experimental import pallas as pl
from jax.experimental.pallas import tpu as pltpu
from jax.sharding import PartitionSpec as P

EPS = 1e-05
LOW = -3.0e38
LANES = 128
TILE = 16
PIECES = (8, 7, 5)
ROWS = 256
TOKEN_BYTES = 17 * 2**20


def assemble_kernel(near_first, gain_ref, *refs):
    target = refs[-1]
    sources = []
    for away, ref in enumerate(refs[:-1]):
        for index in range(ref.shape[0]):
            part = lax.axis_index("vocab") ^ (2 * index + away) if near_first else index
            sources.append((ref, index, part))
    features = refs[0].shape[3]
    for start in range(0, target.shape[3], LANES):
        lanes = slice(start, start + LANES)
        square = sum(
            jnp.sum(jnp.square(ref[at, 0, lanes].astype(jnp.float32)), axis=1, keepdims=True) for ref, at, _ in sources
        )
        scale = lax.rsqrt(square / (features * len(sources)) + EPS)
        for ref, at, part in sources:
            first = pl.multiple_of(part * features, features)
            value = ref[at, 0, lanes].astype(jnp.float32) * scale * gain_ref[:, pl.ds(first, features)]
            target[0, 0, pl.ds(first, features), lanes] = value.T.astype(target.dtype)


def assemble(gain, sources, rows):
    _, count, slots, features = sources[0].shape
    splits = slots // rows
    wide = features * sum(y.shape[0] for y in sources)
    return pl.pallas_call(
        functools.partial(assemble_kernel, len(sources) > 1),
        grid=(count, splits),
        in_specs=[pl.BlockSpec((1, wide), lambda i, j: (0, 0))]
        + [pl.BlockSpec((y.shape[0], 1, rows, features), lambda i, j: (0, i, j, 0)) for y in sources],
        out_specs=pl.BlockSpec((1, 1, wide, rows), lambda i, j: (i, j, 0, 0)),
        out_shape=jax.ShapeDtypeStruct((count, splits, wide, rows), sources[0].dtype),
        compiler_params=pltpu.CompilerParams(vmem_limit_bytes=24 * 2**20),
        cost_estimate=pl.CostEstimate(
            flops=6 * count * splits * rows * wide,
            bytes_accessed=4 * count * splits * rows * wide,
            transcendentals=count * splits * rows,
        ),
    )(gain, *sources)


def stats_kernel(plan, counts, start_ref, lens_ref, owner_ref, *refs):
    out_ref, head, held, logits, ids, order, sems, token_sems = refs[-8:]
    members = []
    for count in counts:
        members.append(refs[:count])
        refs = refs[count:]
    token_refs, id_refs, head_refs, before = members
    splits, _, rows = token_refs[0].shape[1:]
    groups = len(token_refs) * token_refs[0].shape[0]
    width, depth = head.shape[0], head_refs[0].shape[-1]
    real, base = plan.columns()

    copies = []
    for source, first, group in plan.head_parts(head_refs):
        target = head.at[pl.ds(first, source.shape[0]), pl.ds(pl.multiple_of(group * depth, LANES), depth)]
        copies.append(pltpu.make_async_copy(source, target, sems.at[len(copies)]))
    for copy in copies:
        copy.start()

    def one_group(group, live):
        def one_sequence(index, load):
            return load + jnp.where(owner_ref[index] == plan.group(group), lens_ref[index], 0)

        load = lax.fori_loop(0, lens_ref.shape[0], one_sequence, jnp.int32(0))
        for split in range(splits):
            order[live] = group * splits + split
            live = live + jnp.where(start_ref[0] + split * rows < load, 1, 0)
        return live

    live = lax.fori_loop(0, groups, one_group, jnp.int32(0))

    def fetch(step, slot):
        group, split = order[step] // splits, order[step] % splits
        each = token_refs[0].shape[0]
        for index, source in enumerate(token_refs):

            @pl.when(group // each == index)
            def _():
                for first in range(0, held.shape[1], held.shape[1] // 4):
                    part = pl.ds(first, held.shape[1] // 4)
                    pltpu.make_async_copy(
                        source.at[group % each, split, part], held.at[slot, part], token_sems.at[slot]
                    ).start()

    @pl.when(live > 0)
    def _():
        fetch(0, 0)

    out_ref[...] = jnp.zeros_like(out_ref)
    for index, source in enumerate(id_refs):
        places = source[...] - base
        ids[pl.ds(index * source.shape[0], source.shape[0])] = jnp.where(places < real, places, -1)
    for copy in copies:
        copy.wait()

    def body(step, carry):
        slot = lax.rem(step, 2)
        pltpu.make_async_copy(token_refs[0].at[0, 0], held.at[slot], token_sems.at[slot]).wait()

        @pl.when(step + 1 < live)
        def _():
            fetch(step + 1, 1 - slot)

        logits[...] = jnp.dot(head[...], held[slot], preferred_element_type=jnp.float32)

        @pl.when(real < width)
        def _():
            column = lax.broadcasted_iota(jnp.int32, (width - plan.least, rows), 0) + plan.least
            logits[plan.least :] = jnp.where(column < real, logits[plan.least :], LOW)

        block = order[step]
        target = plan.slot(block // splits)
        split = block % splits
        column = lax.broadcasted_iota(jnp.int32, (width, LANES), 0)
        for start in range(0, rows, LANES):
            lanes = slice(start, start + LANES)
            values = logits[:, lanes]
            top = jnp.max(values, axis=0, keepdims=True)
            shifted = jnp.maximum(values - top, -1.0e4)
            expo = jnp.exp(shifted)
            total = jnp.sum(expo, axis=0, keepdims=True)
            weighted = jnp.sum(expo * shifted, axis=0, keepdims=True)
            picked = jnp.sum(jnp.where(column == ids[block, :, lanes], values, 0.0), axis=0, keepdims=True)
            place = pl.ds(pl.multiple_of(split * rows + start, LANES), LANES)
            if before:
                top, total, weighted, picked = joined(
                    [(top, total, weighted, picked), [before[0][target, index : index + 1, place] for index in range(4)]]
                )
            for index, member in enumerate((top, total, weighted, picked)):
                out_ref[target, index : index + 1, place] = member
        return carry

    lax.fori_loop(0, live, body, 0)


def stats(plan, start, seq_lens, seq_owner, tokens, ids, heads, before):
    groups, splits, wide, rows = tokens[0].shape
    groups *= len(tokens)
    width = plan.width
    smem = pl.BlockSpec(memory_space=pltpu.SMEM)
    vmem = pl.BlockSpec(memory_space=pltpu.VMEM)
    anywhere = pl.BlockSpec(memory_space=pltpu.HBM)
    return pl.pallas_call(
        functools.partial(stats_kernel, plan, (len(tokens), len(ids), len(heads), len(before))),
        in_specs=[smem] * 3
        + [anywhere] * len(tokens)
        + [vmem] * len(ids)
        + [anywhere] * len(heads)
        + [vmem] * len(before),
        out_specs=vmem,
        scratch_shapes=[
            pltpu.VMEM((width, wide), jnp.bfloat16),
            pltpu.VMEM((2, wide, rows), jnp.bfloat16),
            pltpu.VMEM((width, rows), jnp.float32),
            pltpu.VMEM((groups * splits, 1, rows), jnp.int32),
            pltpu.SMEM((groups * splits + 1,), jnp.int32),
            pltpu.SemaphoreType.DMA((plan.copies,)),
            pltpu.SemaphoreType.DMA((2,)),
        ],
        out_shape=jax.ShapeDtypeStruct((groups, 4, splits * rows), jnp.float32),
        compiler_params=pltpu.CompilerParams(vmem_limit_bytes=60 * 2**20),
        cost_estimate=pl.CostEstimate(
            flops=groups * splits * rows * wide * width // 8,
            bytes_accessed=wide * width,
            transcendentals=groups * splits * rows * width // 8,
        ),
    )(start, seq_lens, seq_owner, *tokens, *ids, *heads, *before)


class Spread:
    def __init__(self, breadth, groups):
        self.breadth = breadth
        self.cuts = [breadth * index // groups // TILE * TILE for index in range(groups)] + [breadth]
        sizes = [end - start for start, end in zip(self.cuts, self.cuts[1:])]
        self.width, self.least = max(sizes), min(sizes)
        self.copies = 1

    def spread(self, turned):
        turned = jnp.pad(turned, ((0, self.cuts[-2] + self.width - self.breadth), (0, 0)))
        return jnp.stack([turned[start : start + self.width] for start in self.cuts[:-1]])

    def columns(self):
        position = lax.axis_index("dp")
        start, end = 0, self.breadth
        for index, (first, last) in enumerate(zip(self.cuts, self.cuts[1:])):
            start = jnp.where(position == index, first, start)
            end = jnp.where(position == index, last, end)
        return end - start, lax.axis_index("vocab") * self.breadth + start

    def head_parts(self, refs):
        return [(refs[0], 0, 0)]

    def group(self, group):
        return group

    def slot(self, group):
        return group


class Line:
    def __init__(self, breadth, chunk, cuts):
        self.breadth, self.chunk, self.cuts = breadth, chunk, cuts
        self.start = cuts[0][0]
        self.width = self.least = sum(width for _, width in cuts)
        self.copies = 2 + 6 * len(cuts)

    def columns(self):
        hi = lax.axis_index("dp") // 2
        return self.width, lax.axis_index("vocab") * self.breadth + hi * self.chunk + self.start

    def head_parts(self, refs):
        position = lax.axis_index("dp")
        hi, low = position // 2, position % 2
        here = pl.ds(self.start, self.width)
        found = [(refs[0].at[hi, here], 0, 2 * hi + low), (refs[1].at[here], 0, 2 * hi + (low ^ 1))]
        for index, (start, _) in enumerate(self.cuts):
            *mine, other = refs[2 + 4 * index : 6 + 4 * index]
            for step in (1, 2, 3):
                found.append((mine[step - 1], start - self.start, 2 * (hi ^ step) + low))
                found.append((other.at[step - 1], start - self.start, 2 * (hi ^ step) + (low ^ 1)))
        return found

    def slot(self, group):
        hi = lax.axis_index("dp") // 2
        middle = (hi == 1) | (hi == 2)
        return jnp.where(middle & (group >= 2), 5 - group, group)

    def group(self, group):
        position = lax.axis_index("dp")
        return 2 * (position // 2 ^ self.slot(group)) + position % 2


def after(x, *others):
    return lax.optimization_barrier((x, *others))[0]


def joined(members):
    best = functools.reduce(jnp.maximum, [top for top, _, _, _ in members])
    total = weighted = picked = 0.0
    for top, other_total, other_weighted, other_picked in members:
        shift = jnp.maximum(top - best, -1.0e4)
        factor = jnp.exp(shift)
        total += other_total * factor
        weighted += factor * (other_weighted + other_total * shift)
        picked += other_picked
    return best, total, weighted, picked


def merge(members):
    return jnp.stack(joined([[member[..., index, :] for index in range(4)] for member in members]), axis=-2)


def by_collectives(hidden, gain, head, target_ids, seq_lens, seq_owner):
    groups = lax.axis_size("dp")
    parts = lax.axis_size("vocab")
    slots, features = hidden.shape
    depth, breadth = head.shape
    plan = Spread(breadth, groups)
    ids = lax.all_gather(target_ids, "dp", axis=0)

    columns = lax.all_to_all(plan.spread(head.T), "dp", split_axis=0, concat_axis=0, tiled=True)
    columns = columns.transpose(1, 0, 2).reshape(plan.width, groups * depth)

    splits = -(-groups * slots * features * parts * 2 // TOKEN_BYTES)
    while slots % splits or (slots // splits) % LANES:
        splits += 1
    rows = slots // splits

    def score(start):
        piece = lax.dynamic_slice_in_dim(hidden, start, rows)
        x = lax.all_gather(piece, ("vocab", "dp"), axis=0).reshape(parts, groups, rows, features)
        x = assemble(gain, [x], rows)
        wanted = lax.dynamic_slice_in_dim(ids, start, rows, axis=1)[:, None]
        return stats(plan, start[None], seq_lens, seq_owner, [x], [wanted], [columns], [])

    found = lax.map(score, jnp.arange(splits, dtype=jnp.int32) * rows)
    found = found.transpose(1, 2, 0, 3).reshape(groups, 4, slots)
    found = lax.all_to_all(found, "dp", split_axis=0, concat_axis=0, tiled=True)
    mine = lax.all_gather(merge(list(found)), "vocab", axis=0)
    return merge(list(mine))


def by_axes(hidden, gain, head, target_ids, seq_lens, seq_owner):
    groups = lax.axis_size("dp")
    parts = lax.axis_size("vocab")
    tall = groups // 2
    hi = lax.axis_index("dp") // 2
    slots, features = hidden.shape
    depth, breadth = head.shape
    splits = slots // ROWS
    middle = (hi == 1) | (hi == 2)
    chunk = breadth // tall
    ends = [chunk * sum(PIECES[:n]) // sum(PIECES) // TILE * TILE for n in range(len(PIECES))] + [chunk]
    cuts = [(start, end - start) for start, end in zip(ends, ends[1:])]

    def swap_hi(x, step):
        return lax.ppermute(x, "dp", [(g, g ^ (2 * step)) for g in range(groups)])

    def swap_lo(x):
        return lax.ppermute(x, "dp", [(g, g ^ 1) for g in range(groups)])

    def swap_part(x, step):
        return lax.ppermute(x, "vocab", [(v, v ^ step) for v in range(parts)])

    def along(x, moves):
        return lax.ppermute(x, "dp", [(2 * a + side, 2 * b + side) for a, b in moves for side in range(2)])

    code = jnp.stack([target_ids >> 8, target_ids & 255]).astype(hidden.dtype).reshape(2, splits, ROWS)
    code = code.transpose(1, 0, 2).reshape(splits, 2 * ROWS)
    own = jnp.concatenate([hidden, jnp.pad(code, ((0, TILE - splits), (0, features - 2 * ROWS)))])
    near = swap_hi(own, 1)
    cross = along(own, [(1, 2), (2, 1)])
    cross_near = along(near, [(1, 2), (2, 1)])
    out = along(cross, [(1, 0), (2, 3)])
    out_near = along(cross_near, [(1, 0), (2, 3)])

    turned = head.T.reshape(tall, chunk, depth)

    def block(step, start, width):
        return lax.dynamic_slice(turned, (hi ^ step, start, 0), (1, width, depth))[0]

    blocks = [[block(step, *cut) for step in (1, 2, 3)] for cut in cuts]

    def to_hi(piece, *others):
        return [swap_hi(after(y, *others), step) for step, y in enumerate(blocks[piece], 1)]

    def over_x(x):
        return swap_part(x, 2)

    def both(x, y, x_across, y_across):
        return jnp.stack([jnp.stack([x, y]), jnp.stack([x_across, y_across])])

    def ready(half, whole):
        code = half[0, :, slots : slots + splits, : 2 * ROWS].astype(jnp.int32).reshape(2 * splits, 2, ROWS)
        return assemble(gain, [half, whole], ROWS), code[:, :1] * 256 + code[:, 1:]

    def score(pieces, before):
        plan = Line(breadth, chunk, [cuts[piece] for piece in pieces])
        heads = [turned, local_block, *(y for piece in pieces for y in (*sent[piece], across[piece]))]
        return stats(plan, jnp.zeros(1, jnp.int32), seq_lens, seq_owner, tokens, ids, heads, before)

    local_block = swap_lo(block(0, 0, chunk))
    own_across = over_x(own)
    near_across = over_x(after(near, cross, own_across, local_block))
    sent = [to_hi(0, out, cross_near, near_across, *blocks[1], *blocks[2])]
    far = jnp.where(middle, cross, out)
    far_across = over_x(far)
    last = jnp.where(middle, cross_near, out_near)
    last_across = over_x(after(last, *sent[0]))
    sent.append(to_hi(1, *sent[0], far_across))
    front_half = both(own, near, own_across, near_across)
    across = [swap_lo(jnp.stack(sent[0]))]
    front = ready(front_half, swap_part(after(front_half, *sent[1], across[0]), 1))
    back_half = both(far, last, far_across, last_across)
    back = ready(back_half, swap_part(after(back_half, *sent[1], across[0]), 1))
    tokens, ids = zip(front, back)
    waits = (tokens[0], sent[1][1], sent[1][2])
    sent.append([swap_hi(after(y, *sent[1], wait), step) for step, (y, wait) in enumerate(zip(blocks[2], waits), 1)])
    across.append(swap_lo(jnp.stack(sent[1])))
    across.append(swap_lo(after(jnp.stack(sent[2]), across[1])))
    found = score((2,), [score((0, 1), [])])
    mine = merge([found[0]] + [swap_hi(found[step], step) for step in range(1, tall)])
    return merge([mine] + [swap_part(mine, step) for step in range(1, parts)])


def local(hidden, gain, head, target_ids, seq_lens, seq_owner):
    groups = lax.axis_size("dp")
    slots, features = hidden.shape
    owners = jnp.arange(groups, dtype=jnp.int32)
    loads = jnp.sum(jnp.where(seq_owner[:, None] == owners[None, :], seq_lens[:, None], 0), axis=0).astype(jnp.int32)
    fits = (
        (groups, lax.axis_size("vocab")) == (8, 4)
        and slots % ROWS == 0
        and slots // ROWS <= TILE
        and 2 * ROWS <= features
        and head.shape[1] % (groups // 2 * TILE) == 0
    )
    transport = by_axes if fits else by_collectives
    scores = transport(hidden, gain.astype(jnp.float32)[None], head, target_ids, seq_lens, seq_owner)
    top, total, weighted, picked = (scores[index] for index in range(4))
    spread = jnp.log(total)
    logprob = picked - (top + spread)
    entropy = spread - weighted / total
    live = jnp.arange(slots, dtype=jnp.int32) < loads[lax.axis_index("dp")]
    return (jnp.where(live, logprob, 0.0), jnp.where(live, entropy, 0.0))


def solution(mesh):
    return jax.shard_map(
        local,
        mesh=mesh,
        in_specs=(P("dp", "vocab"), P(), P("dp", "vocab"), P("dp"), P(), P()),
        out_specs=(P("dp"), P("dp")),
        check_vma=False,
    )
```
